512 devices in a mesh: wide: 64 (over z, y), narrow: 8 (over x, core).
Axes of the slice: x: 4, y: 4, z: 16, core: 2. Of those that a mesh axis runs over, the one named last changes fastest.
Arguments:
- activations: bfloat16 [192, 2, 8192], P('wide', None, 'narrow'), may hold values from -24 to 24
- norm_gain: float32 [8192], P('narrow'), may hold values from 0.1 to 1.9
- w_query: bfloat16 [8192, 8192], P('narrow', 'wide'), may hold values from -0.0625 to 0.0625
- w_keyval: bfloat16 [8192, 512], P('narrow', 'wide'), may hold values from -0.1875 to 0.1875
- w_out: bfloat16 [8192, 8192], P('wide', 'narrow'), may hold values from -0.0625 to 0.0625
- w_gate: bfloat16 [8192, 32768], P('narrow', 'wide'), may hold values from -0.0625 to 0.0625
- w_up: bfloat16 [8192, 32768], P('narrow', 'wide'), may hold values from -0.0625 to 0.0625
- w_down: bfloat16 [32768, 8192], P('wide', 'narrow'), may hold values from -0.03125 to 0.03125
- key_cache: bfloat16 [192, 2048, 256], P('wide', 'narrow'), may hold values from -240 to 240
- value_cache: bfloat16 [192, 2048, 256], P('wide', 'narrow'), may hold values from -6 to 6
- lengths: int32 [192], P('wide'), may hold values from 1 to 2048, as said below
Outputs:
- mixed: bfloat16 [192, 2, 8192], P('wide', None, 'narrow')
The draws below stay inside these ranges and needn't reach their ends.
Inputs may be any that keep to these rules, and one draw needn't show every extreme that they name: Row r's cache is filled at positions below lengths[r]; in every draw some row is full and some row holds one position.
All inputs are finite; a program needn't handle non-finite values.
Results may differ from the reference program's by a relative error of at most 0.01.
Values may be sent and summed in bfloat16 or wider, within the bound.
No kernel may reach another device: no remote copies, remote signals or barrier semaphores. Data moves between devices by JAX's collectives and lax.ppermute only.
A program may use at most 64 MiB of HBM per device.

```python
import math
import jax
import jax.numpy as jnp
from jax import lax

D = 8192
HEADS = 32
HEAD_DIM = 256
FF = 32768
NEW = 2
ROWS = 192
CACHE_LEN = 2048


def draw_activations(key, part):
    key = jax.random.fold_in(key, 2)
    first_key = jax.random.fold_in(key, 0)
    columns = jnp.exp(jnp.linspace(0.0, math.log(3.0), D, dtype=jnp.float32))
    drawn = jax.random.normal(first_key, (ROWS, NEW, D), jnp.float32) * columns
    return jnp.clip(drawn, -24.0, 24.0).astype(jnp.bfloat16)


def draw_key_cache(key, part):
    key = jax.random.fold_in(key, 1)
    first_key = jax.random.fold_in(key, 0)
    drawn = jnp.clip(3.0 * jax.random.normal(first_key, (ROWS, CACHE_LEN, HEAD_DIM), jnp.float32), -12.0, 12.0)
    return drawn.astype(jnp.bfloat16)


def draw_lengths(key, part):
    key = jax.random.fold_in(key, 3)
    first_key, second_key = jax.random.split(key)
    drawn = jax.random.randint(first_key, (ROWS,), 1, CACHE_LEN + 1, dtype=jnp.int32)
    order = jax.random.permutation(second_key, ROWS)
    drawn = drawn.at[order[0]].set(CACHE_LEN)
    drawn = drawn.at[order[1]].set(1)
    return drawn.astype(jnp.int32)


def levels(own_key, dims, pieces, smallest, largest):
    gain = 1.0
    for axis_at, shards_of in pieces:
        heights = jax.random.uniform(jax.random.fold_in(jax.random.fold_in(own_key, 6), axis_at), (shards_of,), jnp.float32, smallest / len(pieces), largest / len(pieces))
        gain = gain * jnp.repeat(jnp.exp(heights), dims[axis_at] // shards_of).reshape((-1,) + (1,) * (len(dims) - 1 - axis_at))
    return gain


def normal_values(stream_key, shape, deviation, reach, shards=(), kind=jnp.bfloat16):
    values = deviation * jax.random.normal(stream_key, shape, jnp.float32)
    if shards:
        values = values * levels(stream_key, shape, shards, -0.22, 0.18)
    return jnp.clip(values, -reach, reach).astype(kind)


def setup_inputs(seed: int = 0) -> dict:
    streams_of = jax.random.split(jax.random.key(seed), 12)
    return {
        "activations": draw_activations(jax.random.fold_in(streams_of[11], 71), 0),
        "norm_gain": jnp.clip(1.0 + 0.18 * jax.random.normal(streams_of[1], (D,), jnp.float32), 0.1, 1.9),
        "w_query": normal_values(streams_of[2], (D, HEADS * HEAD_DIM), D ** -0.5, 0.0625, ((0, 8), (1, 64))),
        "w_keyval": normal_values(streams_of[3], (D, 2 * HEAD_DIM), (D // 9) ** -0.5, 0.1875, ((0, 8), (1, 64))),
        "w_out": normal_values(streams_of[4], (HEADS * HEAD_DIM, D), (HEADS * HEAD_DIM) ** -0.5, 0.0625, ((0, 64), (1, 8))),
        "w_gate": normal_values(streams_of[5], (D, FF), D ** -0.5, 0.0625, ((0, 8), (1, 64))),
        "w_up": normal_values(streams_of[6], (D, FF), D ** -0.5, 0.0625, ((0, 8), (1, 64))),
        "w_down": normal_values(streams_of[7], (FF, D), FF ** -0.5, 0.03125, ((0, 64), (1, 8))),
        "key_cache": draw_key_cache(jax.random.fold_in(streams_of[11], 71), 0),
        "value_cache": normal_values(streams_of[9], (ROWS, CACHE_LEN, HEAD_DIM), 1.0, 6.0, ((0, 64), (1, 8))),
        "lengths": draw_lengths(jax.random.fold_in(streams_of[11], 71), 0),
    }


eps_norm = 1e-05
masked_score = -1e+30

def attend_row(inputs):
    query_rows, cache_keys, cache_values, new_keys, new_values, length = inputs
    factor = HEAD_DIM ** (-0.5)
    queries = query_rows.astype(jnp.float32)
    cache_scores = jnp.einsum('thd,pd->thp', queries, cache_keys.astype(jnp.float32)) * factor
    usable = (jnp.arange(CACHE_LEN) < length)[None, None, :]
    cache_scores = jnp.where(usable, cache_scores, masked_score)
    own_scores = jnp.einsum('thd,ud->thu', queries, new_keys.astype(jnp.float32)) * factor
    causal = (jnp.arange(NEW)[:, None] >= jnp.arange(NEW)[None, :])[:, None, :]
    own_scores = jnp.where(causal, own_scores, masked_score)
    highest = jnp.maximum(cache_scores.max(-1), own_scores.max(-1))
    cache_weights = jnp.where(usable, jnp.exp(cache_scores - highest[..., None]), 0.0)
    own_weights = jnp.where(causal, jnp.exp(own_scores - highest[..., None]), 0.0)
    weight_sum = cache_weights.sum(-1) + own_weights.sum(-1)
    weighted = jnp.einsum('thp,pd->thd', cache_weights, cache_values.astype(jnp.float32))
    weighted = weighted + jnp.einsum('thu,ud->thd', own_weights, new_values.astype(jnp.float32))
    return (weighted / weight_sum[..., None]).astype(jnp.bfloat16)

def reference(activations, norm_gain, w_query, w_keyval, w_out, w_gate, w_up, w_down, key_cache, value_cache, lengths):
    values_f = activations.astype(jnp.float32)
    centre = lax.optimization_barrier(jnp.sum(values_f, axis=-1, keepdims=True)) / D
    spread = lax.optimization_barrier(jnp.sum(values_f * values_f, axis=-1, keepdims=True)) / D - centre * centre
    normed = ((values_f - centre) * lax.rsqrt(spread + eps_norm) * norm_gain).astype(jnp.bfloat16)
    flat_rows = normed.reshape(ROWS * NEW, D)
    query_all = jnp.dot(flat_rows, w_query, preferred_element_type=jnp.float32).astype(jnp.bfloat16)
    query_all = query_all.reshape(ROWS, NEW, HEADS, HEAD_DIM)
    keyval = jnp.dot(flat_rows, w_keyval, preferred_element_type=jnp.float32).astype(jnp.bfloat16)
    keyval = keyval.reshape(ROWS, NEW, 2 * HEAD_DIM)
    new_keys = keyval[..., :HEAD_DIM]
    new_values = keyval[..., HEAD_DIM:]
    gate_sum = jnp.dot(flat_rows, w_gate, preferred_element_type=jnp.float32)
    up_sum = jnp.dot(flat_rows, w_up, preferred_element_type=jnp.float32)
    hidden = (jax.nn.silu(gate_sum) * up_sum).astype(jnp.bfloat16)
    attended = lax.map(attend_row, (query_all, key_cache, value_cache, new_keys, new_values, lengths))
    attended = attended.reshape(ROWS * NEW, HEADS * HEAD_DIM)
    mixed = values_f.reshape(ROWS * NEW, D)
    mixed = mixed + jnp.dot(attended, w_out, preferred_element_type=jnp.float32)
    mixed = mixed + jnp.dot(hidden, w_down, preferred_element_type=jnp.float32)
    return mixed.astype(jnp.bfloat16).reshape(ROWS, NEW, D)
```

```python
import jax
import jax.numpy as jnp
import numpy as np
from jax import lax
from jax.sharding import Mesh
from jax.sharding import PartitionSpec as P

D = 8192
eps_norm = 1e-05
masked_score = -1e30
bf16 = jnp.bfloat16
f32 = jnp.float32
WIDE = ("z", "y")
NARROW = ("x", "core")


def three_parts(value):
    first = lax.reduce_precision(value, 8, 7)
    rest = value - first
    second = lax.reduce_precision(rest, 8, 7)
    return first, second, lax.reduce_precision(rest - second, 8, 7)


def local(
    activations,
    norm_gain,
    w_query,
    w_keyval,
    w_out,
    w_gate,
    w_up,
    w_down,
    key_cache,
    value_cache,
    lengths,
):
    zs, ys, ns = lax.axis_size("z"), lax.axis_size("y"), lax.axis_size(NARROW)
    ws = zs * ys
    rows, new, width = activations.shape
    toks = rows * new
    every = ws * toks
    head_dim = key_cache.shape[2]
    kv_cols = w_keyval.shape[1]
    lanes = w_query.shape[1]
    heads = ws * lanes // head_dim
    halves = head_dim // lanes
    ffn = w_gate.shape[1]

    values = activations.reshape(toks, width).astype(f32)
    sums = jnp.concatenate([values.sum(-1), (values * values).sum(-1)])
    sums = jnp.pad(sums, (0, 128 - 2 * toks))[None]
    sums = lax.all_gather(sums, NARROW, axis=0, tiled=True).sum(0)
    centre = sums[:toks, None] / D
    spread = sums[toks : 2 * toks, None] / D - centre * centre
    normed = ((values - centre) * lax.rsqrt(spread + eps_norm) * norm_gain).astype(bf16)

    copies = jnp.broadcast_to(jnp.pad(normed, ((0, 8 - toks), (0, 0)))[None], (zs, 8, width))
    column = lax.all_to_all(copies, "z", 0, 0, tiled=True)
    column = column[:, :toks].reshape(zs * toks, width)
    flat = lax.all_gather(column, "y", axis=0, tiled=True)

    gate_up = jnp.dot(flat, jnp.concatenate([w_gate, w_up], axis=1), preferred_element_type=f32)

    query_part = jnp.dot(flat, w_query, preferred_element_type=f32).astype(bf16)
    lane = np.arange(lanes)
    spreader = jnp.asarray((lane[None, :] % kv_cols) == np.arange(kv_cols)[:, None], bf16)
    w_pair = jnp.dot(w_keyval, spreader, preferred_element_type=f32).astype(bf16)
    pair_part = jnp.dot(flat, w_pair, preferred_element_type=f32).astype(bf16)
    keep = (lane[None, :] // kv_cols) == (np.arange(every)[:, None] % toks)
    pair_part = jnp.where(keep, pair_part, jnp.zeros_like(pair_part))
    collect = jnp.asarray(np.arange(ws)[:, None] == (np.arange(every)[None, :] // toks), bf16)
    pair_rows = jnp.dot(collect, pair_part, preferred_element_type=f32).astype(bf16)
    parts = jnp.concatenate([query_part, pair_rows], axis=0)
    parts = lax.all_gather(parts, NARROW, axis=0, tiled=False)
    summed = parts.astype(f32).sum(0).astype(bf16)

    gate_up = lax.psum_scatter(gate_up, NARROW, scatter_dimension=0, tiled=True)

    block = jnp.concatenate(
        [
            summed[:every].reshape(ws, toks, lanes),
            summed[every:][:, None, :],
            jnp.zeros((ws, 8 - toks - 1, lanes), bf16),
        ],
        axis=1,
    )
    block = lax.all_to_all(block.reshape(ys, zs * 8, lanes), "y", 0, 0, tiled=True)
    block = block.reshape(ys, zs, 8, lanes).transpose(1, 0, 2, 3).reshape(zs, ys * 8, lanes)
    block = lax.all_to_all(block, "z", 0, 0, tiled=True)
    block = block.reshape(ws, 8, lanes)

    queries = (
        block[:, :toks]
        .reshape(heads, halves, rows, new, lanes)
        .transpose(2, 3, 0, 1, 4)
        .reshape(rows, new * heads, head_dim)
    )
    pairs = (
        block[:, toks, : toks * kv_cols]
        .reshape(ws, toks, kv_cols)
        .transpose(1, 0, 2)
        .reshape(rows, new, 2 * head_dim)
    )
    new_keys, new_values = pairs[..., :head_dim], pairs[..., head_dim:]
    narrow_index = lax.axis_index(NARROW)
    cache_part = key_cache.shape[1]
    factor = head_dim ** (-0.5)
    positions = narrow_index * cache_part + jnp.arange(cache_part, dtype=jnp.int32)
    usable = (positions[None, :] < lengths[:, None])[:, None, :]
    scores = jnp.einsum("rqd,rpd->rqp", queries, key_cache, preferred_element_type=f32) * factor
    scores = jnp.where(usable, scores, masked_score)
    own = jnp.einsum("rqd,rud->rqu", queries, new_keys, preferred_element_type=f32) * factor
    token_of = np.arange(new * heads) // heads
    causal = (token_of[:, None] >= np.arange(new)[None, :])[None]
    causal = jnp.logical_and(causal, narrow_index == 0)
    own = jnp.where(causal, own, masked_score)
    top = jnp.maximum(scores.max(-1), own.max(-1))
    weights = jnp.where(usable, jnp.exp(scores - top[..., None]), 0.0)
    own_weights = jnp.where(causal, jnp.exp(own - top[..., None]), 0.0)
    total = weights.sum(-1) + own_weights.sum(-1)
    weighted = jnp.einsum("rqp,rpd->rqd", weights.astype(bf16), value_cache, preferred_element_type=f32)
    weighted = weighted + jnp.einsum("rqu,rud->rqd", own_weights, new_values.astype(f32))

    sent = (
        weighted.astype(bf16)
        .reshape(rows, new, heads, halves, lanes)
        .transpose(2, 3, 0, 1, 4)
        .reshape(ws, toks, lanes)
    )
    marks = jnp.stack(three_parts(top) + three_parts(total))
    marks = marks.reshape(6, toks, heads).transpose(2, 0, 1)
    marks = jnp.pad(marks, ((0, 0), (0, 0), (0, 8 - toks))).reshape(heads, 48)
    marks = jnp.pad(marks, ((0, 0), (0, lanes - 48))).astype(bf16)
    marks = jnp.broadcast_to(marks[:, None], (heads, halves, lanes)).reshape(ws, 1, lanes)
    block = jnp.concatenate([sent, marks, jnp.zeros((ws, 8 - toks - 1, lanes), bf16)], axis=1)
    block = lax.all_to_all(block.reshape(zs, ys * 8, lanes), "z", 0, 0, tiled=True)
    block = block.reshape(zs, ys, 8, lanes).transpose(1, 0, 2, 3).reshape(ys, zs * 8, lanes)
    block = lax.all_to_all(block, "y", 0, 0, tiled=True).reshape(ws, 8, lanes)
    parts = jnp.concatenate([block[:, :toks].reshape(every, lanes), block[:, toks]], axis=0)
    parts = lax.all_gather(parts, NARROW, axis=0, tiled=False)
    weighted = parts[:, :every].astype(f32).reshape(ns, ws, toks, lanes)
    marks = parts[:, every:, :48].astype(f32).reshape(ns, ws, 6, 8)[..., :toks]
    top = marks[:, :, 0] + marks[:, :, 1] + marks[:, :, 2]
    total = marks[:, :, 3] + marks[:, :, 4] + marks[:, :, 5]
    scale = jnp.exp(top - top.max(0))
    scale = scale / (total * scale).sum(0)
    attended = (weighted * scale[..., None]).sum(0).reshape(every, lanes).astype(bf16)

    hidden = (jax.nn.silu(gate_up[:, :ffn]) * gate_up[:, ffn:]).astype(bf16)
    hidden = lax.all_gather(hidden, NARROW, axis=0, tiled=True)

    mixed = jnp.dot(attended, w_out, preferred_element_type=f32) + jnp.dot(
        hidden, w_down, preferred_element_type=f32
    )
    mixed = lax.all_to_all(mixed.astype(bf16).reshape(ys, zs * toks, width), "y", 0, 0, tiled=True)
    mixed = mixed.astype(f32).sum(0).astype(bf16).reshape(zs, toks, width)
    mixed = jnp.pad(mixed, ((0, 0), (0, 8 - toks), (0, 0)))
    mixed = lax.all_to_all(mixed, "z", 0, 0, tiled=True)[:, :toks]
    return (values + mixed.astype(f32).sum(0)).astype(bf16).reshape(activations.shape)


def solution(mesh):
    names = ("z", "y", "x", "core")
    split = Mesh(mesh.devices.reshape(16, 4, 4, 2), names)
    return jax.shard_map(
        local,
        mesh=split,
        in_specs=(
            P(WIDE, None, NARROW),
            P(NARROW),
            P(NARROW, WIDE),
            P(NARROW, WIDE),
            P(WIDE, NARROW),
            P(NARROW, WIDE),
            P(NARROW, WIDE),
            P(WIDE, NARROW),
            P(WIDE, NARROW, None),
            P(WIDE, NARROW, None),
            P(WIDE),
        ),
        out_specs=P(WIDE, None, NARROW),
        check_vma=False,
    )
```

```python
import jax
import jax.numpy as jnp
import numpy as np
from jax import lax
from jax.sharding import Mesh
from jax.sharding import PartitionSpec as P

D = 8192
eps_norm = 1e-05
masked_score = -1e30
bf16 = jnp.bfloat16
f32 = jnp.float32
WIDE = ("z", "y")
NARROW = ("x", "core")


def three_parts(value):
    first = lax.reduce_precision(value, 8, 7)
    rest = value - first
    second = lax.reduce_precision(rest, 8, 7)
    return first, second, lax.reduce_precision(rest - second, 8, 7)


def local(
    activations,
    norm_gain,
    w_query,
    w_keyval,
    w_out,
    w_gate,
    w_up,
    w_down,
    key_cache,
    value_cache,
    lengths,
):
    zs, ys, ns = lax.axis_size("z"), lax.axis_size("y"), lax.axis_size(NARROW)
    ws = zs * ys
    rows, new, width = activations.shape
    toks = rows * new
    mine = zs * toks
    head_dim = key_cache.shape[2]
    kv_cols = w_keyval.shape[1]
    lanes = w_query.shape[1]
    heads = ws * lanes // head_dim
    cols = ys * lanes
    pair_cols = ys * kv_cols
    per_z = cols // head_dim
    ffn = w_gate.shape[1]

    values = activations.reshape(toks, width).astype(f32)
    sums = jnp.concatenate([values.sum(-1), (values * values).sum(-1)])
    sums = jnp.pad(sums, (0, 128 - 2 * toks))[None]
    sums = lax.all_gather(sums, NARROW, axis=0, tiled=True).sum(0)
    centre = sums[:toks, None] / D
    spread = sums[toks : 2 * toks, None] / D - centre * centre
    normed = ((values - centre) * lax.rsqrt(spread + eps_norm) * norm_gain).astype(bf16)

    w_first = lax.all_gather(jnp.concatenate([w_query, w_keyval], axis=1), "y", axis=0, tiled=False)
    w_last = lax.all_gather(w_out, "y", axis=0, tiled=True)

    packed = normed.reshape(toks * width // 128, 128)
    copies = jnp.broadcast_to(packed[None], (zs,) + packed.shape)
    column = lax.all_to_all(copies, "z", 0, 0, tiled=True).reshape(mine, width)

    flat = lax.all_gather(column, "y", axis=0, tiled=True)
    gate_up = jnp.dot(flat, jnp.concatenate([w_gate, w_up], axis=1), preferred_element_type=f32)
    column, gate_up = lax.optimization_barrier((column, gate_up))
    gate_up = lax.psum_scatter(gate_up, NARROW, scatter_dimension=0, tiled=True)

    query_part = jnp.concatenate(
        [jnp.dot(column, w_first[k, :, :lanes], preferred_element_type=f32) for k in range(ys)], axis=1
    ).astype(bf16)
    lane = np.arange(cols)
    spreader = jnp.asarray(
        (lane[None, :] % pair_cols == np.arange(pair_cols)[:, None]) & (lane[None, :] < toks * pair_cols), bf16
    )
    w_pair = jnp.concatenate([w_first[k, :, lanes:] for k in range(ys)], axis=1)
    w_pair = jnp.dot(w_pair, spreader, preferred_element_type=f32).astype(bf16)
    pair_part = jnp.dot(column, w_pair, preferred_element_type=f32).astype(bf16)
    keep = (lane[None, :] // pair_cols) == (np.arange(mine)[:, None] % toks)
    pair_part = jnp.where(keep, pair_part, jnp.zeros_like(pair_part))
    collect = jnp.asarray(np.arange(zs)[:, None] == (np.arange(mine)[None, :] // toks), bf16)
    pair_rows = jnp.dot(collect, pair_part, preferred_element_type=f32).astype(bf16)
    parts = jnp.concatenate([query_part, pair_rows], axis=0)
    parts = lax.all_gather(parts, NARROW, axis=0, tiled=False)
    summed = parts.astype(f32).sum(0).astype(bf16)
    block = jnp.concatenate(
        [
            summed[:mine].reshape(zs, toks, cols),
            summed[mine:][:, None, :],
            jnp.zeros((zs, 8 - toks - 1, cols), bf16),
        ],
        axis=1,
    )
    block = lax.all_to_all(block, "z", 0, 0, tiled=True)

    queries = (
        block[:, :toks]
        .reshape(zs, rows, new, per_z, head_dim)
        .transpose(1, 2, 0, 3, 4)
        .reshape(rows, new * heads, head_dim)
    )
    pairs = (
        block[:, toks, : toks * pair_cols]
        .reshape(zs, toks, pair_cols)
        .transpose(1, 0, 2)
        .reshape(rows, new, 2 * head_dim)
    )
    new_keys, new_values = pairs[..., :head_dim], pairs[..., head_dim:]
    narrow_index = lax.axis_index(NARROW)
    cache_part = key_cache.shape[1]
    factor = head_dim ** (-0.5)
    positions = narrow_index * cache_part + jnp.arange(cache_part, dtype=jnp.int32)
    usable = (positions[None, :] < lengths[:, None])[:, None, :]
    scores = jnp.einsum("rqd,rpd->rqp", queries, key_cache, preferred_element_type=f32) * factor
    scores = jnp.where(usable, scores, masked_score)
    own = jnp.einsum("rqd,rud->rqu", queries, new_keys, preferred_element_type=f32) * factor
    token_of = np.arange(new * heads) // heads
    causal = (token_of[:, None] >= np.arange(new)[None, :])[None]
    causal = jnp.logical_and(causal, narrow_index == 0)
    own = jnp.where(causal, own, masked_score)
    top = jnp.maximum(scores.max(-1), own.max(-1))
    weights = jnp.where(usable, jnp.exp(scores - top[..., None]), 0.0)
    own_weights = jnp.where(causal, jnp.exp(own - top[..., None]), 0.0)
    total = weights.sum(-1) + own_weights.sum(-1)
    weighted = jnp.einsum("rqp,rpd->rqd", weights.astype(bf16), value_cache, preferred_element_type=f32)
    weighted = weighted + jnp.einsum("rqu,rud->rqd", own_weights, new_values.astype(f32))

    sent = (
        weighted.astype(bf16)
        .reshape(rows, new, zs, per_z, head_dim)
        .transpose(2, 0, 1, 3, 4)
        .reshape(zs, toks, cols)
    )
    marks = jnp.stack(three_parts(top) + three_parts(total)).astype(bf16)
    marks = marks.reshape(6, toks, zs, per_z).transpose(2, 3, 0, 1)
    marks = jnp.pad(marks, ((0, 0), (0, 0), (0, 0), (0, 8 - toks))).reshape(zs, per_z, 48)
    marks = jnp.pad(marks, ((0, 0), (0, 0), (0, head_dim - 48))).reshape(zs, 1, cols)
    block = jnp.concatenate([sent, marks, jnp.zeros((zs, 8 - toks - 1, cols), bf16)], axis=1)
    block = lax.all_to_all(block, "z", 0, 0, tiled=True)
    parts = jnp.concatenate([block[:, :toks].reshape(mine, cols), block[:, toks]], axis=0)
    parts = lax.all_gather(parts, NARROW, axis=0, tiled=False)
    weighted = parts[:, :mine].astype(f32).reshape(ns, zs, toks, per_z, head_dim)
    marks = parts[:, mine:].astype(f32).reshape(ns, zs, per_z, head_dim)[..., :48]
    marks = marks.reshape(ns, zs, per_z, 6, 8)[..., :toks].transpose(3, 0, 1, 4, 2)
    top = marks[0] + marks[1] + marks[2]
    total = marks[3] + marks[4] + marks[5]
    scale = jnp.exp(top - top.max(0))
    scale = scale / (total * scale).sum(0)
    attended = (weighted * scale[..., None]).sum(0).reshape(mine, cols).astype(bf16)
    mixed = jnp.dot(attended, w_last, preferred_element_type=f32)

    hidden = (jax.nn.silu(gate_up[:, :ffn]) * gate_up[:, ffn:]).astype(bf16)
    hidden = lax.all_gather(hidden, NARROW, axis=0, tiled=True)
    down = jnp.dot(hidden, w_down, preferred_element_type=f32).astype(bf16)
    down = lax.all_to_all(down.reshape(ys, mine, width), "y", 0, 0, tiled=True)
    mixed = mixed + down.astype(f32).sum(0)

    mixed = mixed.astype(bf16).reshape(zs, toks * width // 128, 128)
    mixed = lax.all_to_all(mixed, "z", 0, 0, tiled=True)
    mixed = mixed.astype(f32).sum(0).reshape(toks, width)
    return (values + mixed).astype(bf16).reshape(activations.shape)


def solution(mesh):
    names = ("z", "y", "x", "core")
    split = Mesh(mesh.devices.reshape(16, 4, 4, 2), names)
    return jax.shard_map(
        local,
        mesh=split,
        in_specs=(
            P(WIDE, None, NARROW),
            P(NARROW),
            P(NARROW, WIDE),
            P(NARROW, WIDE),
            P(WIDE, NARROW),
            P(NARROW, WIDE),
            P(NARROW, WIDE),
            P(WIDE, NARROW),
            P(WIDE, NARROW, None),
            P(WIDE, NARROW, None),
            P(WIDE),
        ),
        out_specs=P(WIDE, None, NARROW),
        check_vma=False,
    )
```

```python
import functools

import jax
import jax.numpy as jnp
import numpy as np
from jax import lax
from jax.experimental import pallas as pl
from jax.experimental.pallas import tpu as pltpu
from jax.sharding import Mesh
from jax.sharding import PartitionSpec as P

D = 8192
eps_norm = 1e-05
masked_score = -1e30
bf16 = jnp.bfloat16
f32 = jnp.float32
vmem = pl.BlockSpec(memory_space=pltpu.VMEM)
anywhere = pl.BlockSpec(memory_space=pl.ANY)
WIDE = ("z", "y")
NARROW = ("x", "core")


def three_parts(value):
    first = lax.reduce_precision(value, 8, 7)
    rest = value - first
    second = lax.reduce_precision(rest, 8, 7)
    return first, second, lax.reduce_precision(rest - second, 8, 7)


def iota(shape, axis):
    return lax.broadcasted_iota(jnp.int32, shape, axis)


def first_kernel(toks, column_ref, source_ref, parts_ref, weights_ref, sems):
    mine, width = column_ref.shape
    ys, _, lanes = weights_ref.shape
    cols = ys * lanes
    chunks = width // lanes
    copies = [pltpu.make_async_copy(source_ref.at[k], weights_ref.at[k], sems.at[k]) for k in range(ys)]
    for copy in copies:
        copy.start()
    column = column_ref[...]
    pairs = []
    for k in range(ys):
        copies[k].wait()
        query = jnp.dot(column, weights_ref[k, :width], preferred_element_type=f32)
        parts_ref[:mine, k * lanes : (k + 1) * lanes] = query.astype(bf16)
        rows = weights_ref[k, width:].astype(f32)
        count = rows.shape[0] // chunks
        pairs.append(jnp.concatenate([rows[j * count : (j + 1) * count] for j in range(chunks)], axis=1))
    pairs = jnp.concatenate(pairs, axis=0).astype(bf16)
    count = pairs.shape[0]
    pairs = lax.dot_general(column, pairs, (((1,), (1,)), ((), ())), preferred_element_type=f32).astype(bf16)
    at = iota((count, cols), 1)
    spread = jnp.where((lax.rem(at, count) == iota((count, cols), 0)) & (at < toks * count), 1.0, 0.0)
    pairs = jnp.dot(pairs, spread.astype(bf16), preferred_element_type=f32)
    start = lax.rem(iota((mine, cols), 0), toks) * count
    at = iota((mine, cols), 1)
    pairs = jnp.where((at >= start) & (at < start + count), pairs, 0.0).astype(bf16)
    start = iota((mine // toks, mine), 0) * toks
    at = iota((mine // toks, mine), 1)
    collect = jnp.where((at >= start) & (at < start + toks), 1.0, 0.0).astype(bf16)
    parts_ref[mine:] = jnp.dot(collect, pairs, preferred_element_type=f32).astype(bf16)


def second_kernel(toks, gate_up_ref, parts_ref, hidden_ref, block_ref):
    ns, rows, cols = parts_ref.shape
    ffn = hidden_ref.shape[1]
    gate = gate_up_ref[0, :, :ffn].astype(f32)
    up = gate_up_ref[0, :, ffn:].astype(f32)
    total = parts_ref[0].astype(f32)
    for n in range(1, ns):
        gate = gate + gate_up_ref[n, :, :ffn].astype(f32)
        up = up + gate_up_ref[n, :, ffn:].astype(f32)
        total = total + parts_ref[n].astype(f32)
    hidden_ref[...] = (gate / (1.0 + jnp.exp(-gate)) * up).astype(bf16)
    shape = (block_ref.shape[0], rows)
    zs = shape[0] // 8
    to, at = iota(shape, 0), iota(shape, 1)
    row = lax.rem(to, 8)
    z = (to - row) // 8
    take = ((row < toks) & (at == z * toks + row)) | ((row == toks) & (at == zs * toks + z))
    take = jnp.where(take, 1.0, 0.0).astype(bf16)
    block_ref[...] = jnp.dot(take, total.astype(bf16), preferred_element_type=f32).astype(bf16)


def last_kernel(toks, per_z, parts_ref, source_ref, down_ref, mixed_ref, weights_ref, sem):
    ns, rows, cols = parts_ref.shape
    mine = mixed_ref.shape[0]
    zs = rows - mine
    copy = pltpu.make_async_copy(source_ref, weights_ref, sem)
    copy.start()
    head = cols // per_z
    shape = (ns * mine, ns * zs)
    start = iota(shape, 1) * toks
    at = iota(shape, 0)
    expand = jnp.where((at >= start) & (at < start + toks), 1.0, 0.0).astype(bf16)
    shape = (ns * mine, 128)
    at = iota(shape, 1)
    own = (lax.rem(at, 8) == lax.rem(iota(shape, 0), toks)) & (at < 48)
    at = iota((128, 128), 0)
    pick_top = jnp.where(at < 24, 1.0, 0.0).astype(bf16)
    pick_total = jnp.where((at >= 24) & (at < 48), 1.0, 0.0).astype(bf16)
    mixed = down_ref[...].astype(f32)
    for k in range(per_z):
        marks = jnp.concatenate([parts_ref[n, mine:, k * head : k * head + 128] for n in range(ns)], axis=0)
        marks = jnp.dot(expand, marks, preferred_element_type=f32)
        marks = jnp.where(own, marks, 0.0).astype(bf16)
        tops = jnp.dot(marks, pick_top, preferred_element_type=f32)
        totals = jnp.dot(marks, pick_total, preferred_element_type=f32)
        tops = [tops[n * mine : (n + 1) * mine] for n in range(ns)]
        top = tops[0]
        for n in range(1, ns):
            top = jnp.maximum(top, tops[n])
        total = jnp.zeros((mine, 128), f32)
        weighted = jnp.zeros((mine, head), f32)
        for n in range(ns):
            scale = jnp.exp(tops[n] - top)
            total = total + totals[n * mine : (n + 1) * mine] * scale
            scale = jnp.concatenate([scale] * (head // 128), axis=1)
            weighted = weighted + parts_ref[n, :mine, k * head : (k + 1) * head].astype(f32) * scale
        total = jnp.concatenate([total] * (head // 128), axis=1)
        attended = (weighted / total).astype(bf16)
        if k == 0:
            copy.wait()
        mixed = mixed + jnp.dot(
            attended, weights_ref[k * head : (k + 1) * head], preferred_element_type=f32
        )
    mixed_ref[...] = mixed.astype(bf16)


def local(
    activations,
    norm_gain,
    w_query,
    w_keyval,
    w_out,
    w_gate,
    w_up,
    w_down,
    key_cache,
    value_cache,
    lengths,
):
    zs, ys, ns = lax.axis_size("z"), lax.axis_size("y"), lax.axis_size(NARROW)
    ws = zs * ys
    rows, new, width = activations.shape
    toks = rows * new
    mine = zs * toks
    head_dim = key_cache.shape[2]
    kv_cols = w_keyval.shape[1]
    lanes = w_query.shape[1]
    heads = ws * lanes // head_dim
    cols = ys * lanes
    pair_cols = ys * kv_cols
    per_z = cols // head_dim
    ffn = w_gate.shape[1]

    values = activations.reshape(toks, width).astype(f32)
    sums = jnp.concatenate([values.sum(-1), (values * values).sum(-1)])
    sums = jnp.pad(sums, (0, 128 - 2 * toks))[None]
    sums = lax.all_gather(sums, NARROW, axis=0, tiled=True).sum(0)
    centre = sums[:toks, None] / D
    spread = sums[toks : 2 * toks, None] / D - centre * centre
    normed = ((values - centre) * lax.rsqrt(spread + eps_norm) * norm_gain).astype(bf16)

    chunks = width // lanes
    pair_lanes = w_keyval.T.reshape(kv_cols, chunks, lanes).transpose(1, 0, 2).reshape(chunks * kv_cols, lanes)
    w_first = lax.all_gather(jnp.concatenate([w_query, pair_lanes], axis=0), "y", axis=0, tiled=False)
    w_last = lax.all_gather(w_out, "y", axis=0, tiled=True)
    w_hidden = lax.optimization_barrier(jnp.concatenate([w_gate, w_up], axis=1))

    packed = normed.reshape(toks * width // 128, 128)
    copies = jnp.broadcast_to(packed[None], (zs,) + packed.shape)
    column = lax.all_to_all(copies, "z", 0, 0, tiled=True).reshape(mine, width)

    flat = lax.all_gather(column, "y", axis=0, tiled=True)
    gate_up = jnp.dot(flat, w_hidden, preferred_element_type=f32).astype(bf16)
    column, gate_up = lax.optimization_barrier((column, gate_up))
    gate_up = lax.all_to_all(gate_up.reshape(ns, -1, 2 * ffn), NARROW, 0, 0, tiled=True)

    parts = pl.pallas_call(
        functools.partial(first_kernel, toks),
        out_shape=jax.ShapeDtypeStruct((mine + zs, cols), bf16),
        in_specs=[vmem, anywhere],
        out_specs=vmem,
        scratch_shapes=[pltpu.VMEM(w_first.shape, bf16), pltpu.SemaphoreType.DMA((ys,))],
        compiler_params=pltpu.CompilerParams(vmem_limit_bytes=24 * 2**20),
        cost_estimate=pl.CostEstimate(flops=2 * mine * width * cols, bytes_accessed=2 * 2**20, transcendentals=0),
        name="first",
    )(column, w_first)
    parts = lax.all_gather(parts, NARROW, axis=0, tiled=False)
    hidden, block = pl.pallas_call(
        functools.partial(second_kernel, toks),
        out_shape=(
            jax.ShapeDtypeStruct((gate_up.shape[1], ffn), bf16),
            jax.ShapeDtypeStruct((zs * 8, cols), bf16),
        ),
        in_specs=[vmem, vmem],
        out_specs=(vmem, vmem),
        compiler_params=pltpu.CompilerParams(vmem_limit_bytes=24 * 2**20),
        cost_estimate=pl.CostEstimate(flops=2**24, bytes_accessed=2 * 2**20, transcendentals=0),
        name="second",
    )(gate_up, parts)
    block = lax.all_to_all(block.reshape(zs, 8, cols), "z", 0, 0, tiled=True)

    queries = (
        block[:, :toks]
        .reshape(zs, rows, new, per_z, head_dim)
        .transpose(1, 2, 0, 3, 4)
        .reshape(rows, new * heads, head_dim)
    )
    pairs = (
        block[:, toks, : toks * pair_cols]
        .reshape(zs, toks, pair_cols)
        .transpose(1, 0, 2)
        .reshape(rows, new, 2 * head_dim)
    )
    new_keys, new_values = pairs[..., :head_dim], pairs[..., head_dim:]
    narrow_index = lax.axis_index(NARROW)
    cache_part = key_cache.shape[1]
    factor = head_dim ** (-0.5)
    positions = narrow_index * cache_part + jnp.arange(cache_part, dtype=jnp.int32)
    usable = (positions[None, :] < lengths[:, None])[:, None, :]
    scores = jnp.einsum("rqd,rpd->rqp", queries, key_cache, preferred_element_type=f32) * factor
    scores = jnp.where(usable, scores, masked_score)
    own = jnp.einsum("rqd,rud->rqu", queries, new_keys, preferred_element_type=f32) * factor
    token_of = np.arange(new * heads) // heads
    causal = (token_of[:, None] >= np.arange(new)[None, :])[None]
    causal = jnp.logical_and(causal, narrow_index == 0)
    own = jnp.where(causal, own, masked_score)
    top = jnp.maximum(scores.max(-1), own.max(-1))
    weights = jnp.where(usable, jnp.exp(scores - top[..., None]), 0.0)
    own_weights = jnp.where(causal, jnp.exp(own - top[..., None]), 0.0)
    total = weights.sum(-1) + own_weights.sum(-1)
    weighted = jnp.einsum("rqp,rpd->rqd", weights.astype(bf16), value_cache, preferred_element_type=f32)
    weighted = weighted + jnp.einsum("rqu,rud->rqd", own_weights, new_values.astype(f32))

    sent = (
        weighted.astype(bf16)
        .reshape(rows, new, zs, per_z, head_dim)
        .transpose(2, 0, 1, 3, 4)
        .reshape(zs, toks, cols)
    )
    marks = jnp.stack(three_parts(top) + three_parts(total)).astype(bf16)
    marks = marks.reshape(6, toks, zs, per_z).transpose(2, 3, 0, 1)
    marks = jnp.pad(marks, ((0, 0), (0, 0), (0, 0), (0, 8 - toks))).reshape(zs, per_z, 48)
    marks = jnp.pad(marks, ((0, 0), (0, 0), (0, head_dim - 48))).reshape(zs, 1, cols)
    block = jnp.concatenate([sent, marks, jnp.zeros((zs, 8 - toks - 1, cols), bf16)], axis=1)
    block = lax.all_to_all(block, "z", 0, 0, tiled=True)
    parts = jnp.concatenate([block[:, :toks].reshape(mine, cols), block[:, toks]], axis=0)
    parts = lax.all_gather(parts, NARROW, axis=0, tiled=False)
    hidden = lax.all_gather(hidden, NARROW, axis=0, tiled=True)
    down = jnp.dot(hidden, w_down, preferred_element_type=f32).astype(bf16)
    down = lax.psum_scatter(down, "y", scatter_dimension=0, tiled=True)

    mixed = pl.pallas_call(
        functools.partial(last_kernel, toks, per_z),
        out_shape=jax.ShapeDtypeStruct((mine, width), bf16),
        in_specs=[vmem, anywhere, vmem],
        out_specs=vmem,
        scratch_shapes=[pltpu.VMEM(w_last.shape, bf16), pltpu.SemaphoreType.DMA],
        compiler_params=pltpu.CompilerParams(vmem_limit_bytes=24 * 2**20),
        cost_estimate=pl.CostEstimate(
            flops=2 * mine * width * cols, bytes_accessed=3 * 2**20, transcendentals=0
        ),
        name="last",
    )(parts, w_last, down)
    mixed = mixed.reshape(zs, toks * width // 128, 128)
    mixed = lax.all_to_all(mixed, "z", 0, 0, tiled=True)
    mixed = mixed.astype(f32).sum(0).reshape(toks, width)
    return (values + mixed).astype(bf16).reshape(activations.shape)


def solution(mesh):
    names = ("z", "y", "x", "core")
    split = Mesh(mesh.devices.reshape(16, 4, 4, 2), names)
    return jax.shard_map(
        local,
        mesh=split,
        in_specs=(
            P(WIDE, None, NARROW),
            P(NARROW),
            P(NARROW, WIDE),
            P(NARROW, WIDE),
            P(WIDE, NARROW),
            P(NARROW, WIDE),
            P(NARROW, WIDE),
            P(WIDE, NARROW),
            P(WIDE, NARROW, None),
            P(WIDE, NARROW, None),
            P(WIDE),
        ),
        out_specs=P(WIDE, None, NARROW),
        check_vma=False,
    )
```

```python
import functools

import jax
import jax.numpy as jnp
import numpy as np
from jax import lax
from jax.experimental import pallas as pl
from jax.experimental.pallas import tpu as pltpu
from jax.sharding import Mesh
from jax.sharding import PartitionSpec as P

D = 8192
eps_norm = 1e-05
masked_score = -1e30
bf16 = jnp.bfloat16
f32 = jnp.float32
vmem = pl.BlockSpec(memory_space=pltpu.VMEM)
hbm = pl.BlockSpec(memory_space=pltpu.HBM)
smem = pl.BlockSpec(memory_space=pltpu.SMEM)
WIDE = ("z", "y")
NARROW = ("x", "core")


def three_parts(value):
    first = lax.reduce_precision(value, 8, 7)
    rest = value - first
    second = lax.reduce_precision(rest, 8, 7)
    return first, second, lax.reduce_precision(rest - second, 8, 7)


def iota(shape, axis):
    return lax.broadcasted_iota(jnp.int32, shape, axis)


def parts_of(value, count):
    found = []
    for _ in range(count):
        found.append(value.astype(bf16).astype(f32))
        value = value - found[-1]
    return found


def gain_rows(gain_ref):
    shape = (8, gain_ref.shape[1])
    rows = jnp.zeros(shape, f32)
    for k, part in enumerate(parts_of(gain_ref[...], 3)):
        rows = jnp.where(iota(shape, 0) == k, part, rows)
    return rows.astype(bf16)


def centred(tokens_ref, gain_ref):
    width = tokens_ref.shape[1]
    tokens = tokens_ref[...]
    mean = tokens.astype(f32).sum(1, keepdims=True) * (1.0 / width)
    return ((tokens.astype(f32) - mean) * gain_ref[...]).astype(bf16)


def across(left, right):
    return lax.dot_general(left, right, (((1,), (1,)), ((), ())), preferred_element_type=f32)


def hidden_kernel(tokens_ref, gain_ref, gate_ref, up_ref, sums_ref, notes_ref):
    ffn = gate_ref.shape[1]
    count, width = tokens_ref.shape
    ready = centred(tokens_ref, gain_ref)
    gains = gain_rows(gain_ref)
    sums_ref[:, :ffn] = jnp.dot(ready, gate_ref[...], preferred_element_type=f32).astype(bf16)
    sums_ref[:, ffn:] = jnp.dot(ready, up_ref[...], preferred_element_type=f32).astype(bf16)
    tokens = tokens_ref[...].astype(f32)
    notes_ref[...] = jnp.zeros_like(notes_ref)
    for k, values in enumerate((tokens, tokens * tokens)):
        total = jnp.broadcast_to(values.sum(1, keepdims=True), (count, 128))
        for j in range(0, count, 128):
            notes_ref[k : k + 1, j : j + 128] = total[j : j + 128].T[0:1]
    for k, ref in enumerate((gate_ref, up_ref)):
        product = jnp.dot(gains, ref[...], preferred_element_type=f32)
        notes_ref[2:3, k * ffn : (k + 1) * ffn] = product.sum(0, keepdims=True)


def first_kernel(toks, column_ref, gain_ref, notes_ref, source_ref, parts_ref, weights_ref, sems):
    mine, width = column_ref.shape
    ys, _, lanes = weights_ref.shape
    cols = ys * lanes
    half = cols // 2
    zs = mine // toks
    chunks = width // lanes
    copies = [pltpu.make_async_copy(source_ref.at[k], weights_ref.at[k], sems.at[k]) for k in range(ys)]
    for copy in copies:
        copy.start()
    column = centred(column_ref, gain_ref)
    gains = gain_rows(gain_ref)
    pairs, products = [], []
    for k in range(ys):
        copies[k].wait()
        query = jnp.dot(column, weights_ref[k, :width], preferred_element_type=f32)
        parts_ref[:mine, k * lanes : (k + 1) * lanes] = query.astype(bf16)
        products.append(jnp.dot(gains, weights_ref[k, :width], preferred_element_type=f32))
        rows = weights_ref[k, width:].astype(f32)
        count = rows.shape[0] // chunks
        pairs.append(jnp.concatenate([rows[j * count : (j + 1) * count] for j in range(chunks)], axis=1))
    pairs = jnp.concatenate(pairs, axis=0)
    count = pairs.shape[0]
    pairs = jnp.concatenate([pairs, jnp.zeros((128 - count, width), f32)], axis=0).astype(bf16)
    pair_products = across(gains, pairs).sum(0, keepdims=True)
    pairs = across(column, pairs).astype(bf16)
    at = iota((128, half), 1)
    spread = jnp.where((lax.rem(at, count) == iota((128, half), 0)) & (at < toks * count), 1.0, 0.0)
    pairs = jnp.dot(pairs, spread.astype(bf16), preferred_element_type=f32)
    start = lax.rem(iota((mine, half), 0), toks) * count
    at = iota((mine, half), 1)
    pairs = jnp.where((at >= start) & (at < start + count), pairs, 0.0).astype(bf16)
    start = iota((zs, mine), 0) * toks
    at = iota((zs, mine), 1)
    collect = jnp.where((at >= start) & (at < start + toks), 1.0, 0.0).astype(bf16)
    pairs = jnp.dot(collect, pairs, preferred_element_type=f32)

    row = iota((zs, half), 0)
    beside = jnp.zeros((zs, half), f32)
    for j in range(4):
        high, low = parts_of(notes_ref[2:3, j * half : (j + 1) * half], 2)
        beside = jnp.where(row == j, high, jnp.where(row == 4 + j, low, beside))
    parts_ref[mine : mine + zs] = jnp.concatenate([pairs, beside], axis=1).astype(bf16)

    row = iota((8, cols), 0)
    tail = jnp.zeros((8, cols), f32)
    for k, part in enumerate(parts_of(notes_ref[0:1, :cols], 3) + parts_of(notes_ref[1:2, :cols], 3)):
        tail = jnp.where(row == k, part, tail)
    products = jnp.concatenate(products, axis=1).sum(0, keepdims=True)
    for k, part in enumerate(parts_of(products, 2)):
        tail = jnp.where(row == 6 + k, part, tail)
    pair_products = jnp.concatenate([jnp.zeros((1, cols - 128), f32), pair_products], axis=1)
    for k, part in enumerate(parts_of(pair_products, 2)):
        tail = jnp.where((row == k) & (iota((8, cols), 1) >= cols - 128), part, tail)
    parts_ref[mine + zs :] = tail.astype(bf16)


def second_kernel(toks, where_ref, sums_ref, parts_ref, hidden_ref, block_ref):
    ns, rows, cols = parts_ref.shape
    ffn = hidden_ref.shape[1]
    half = cols // 2
    zs = block_ref.shape[0] // 8
    mine = zs * toks
    width = 2 * ffn
    tails = jnp.concatenate([parts_ref[n, mine + zs :].astype(f32) for n in range(ns)], axis=0).astype(bf16)
    besides = jnp.concatenate([parts_ref[n, mine : mine + zs, half:] for n in range(ns)], axis=0)
    every = cols - 128

    def pick(shape, group, mask):
        frm, to = iota(shape, 0), iota(shape, 1)
        kind = frm & 7
        same = lax.shift_right_logical(frm, 3) == lax.shift_right_logical(to, group)
        return jnp.where(same & (kind < 3) & mask(to), 1.0, 0.0).astype(bf16)

    def norm(first, count):
        shape = (count, every)
        select = jnp.where(iota(shape, 1) == iota(shape, 0) + first, 1.0, 0.0).astype(bf16)
        own = across(select, tails[:, :every]).astype(bf16)
        kind = iota((ns * 8, 128), 0) & 7
        total = jnp.dot(own, jnp.where(kind < 3, 1.0, 0.0).astype(bf16), preferred_element_type=f32)
        centre = total * (1.0 / D)
        total = jnp.dot(
            own, jnp.where((kind >= 3) & (kind < 6), 1.0, 0.0).astype(bf16), preferred_element_type=f32
        )
        spread = total * (1.0 / D) - centre * centre
        return own, centre, lax.rsqrt(spread + eps_norm)

    def shift(own, centre, group, mask, table):
        shape = (ns * 8, table.shape[0])
        means = jnp.dot(own, pick(shape, group, mask), preferred_element_type=f32) * (1.0 / width)
        shape = (own.shape[0], table.shape[0])
        means = jnp.where(mask(iota(shape, 1)), means - centre[:, : shape[1]], 0.0)
        high, low = parts_of(means, 2)
        return jnp.dot(high.astype(bf16), table, preferred_element_type=f32) + jnp.dot(
            low.astype(bf16), table, preferred_element_type=f32
        )

    count = hidden_ref.shape[0]
    own, centre, scale = norm(where_ref[1] * count, count)
    scale = jnp.concatenate([scale] * (half // 128), axis=1)
    for j in range(2):
        both = []
        for k in (j, j + 2):
            at = slice(k * half, (k + 1) * half)
            total = sums_ref[0, :, at].astype(f32)
            for n in range(1, ns):
                total = total + sums_ref[n, :, at].astype(f32)
            total = total + shift(
                own, centre, 4, lambda to, k=k: ((to & 15) == k) | ((to & 15) == k + 4), besides
            )
            both.append(total * scale)
        gate, up = both
        hidden_ref[:, j * half : (j + 1) * half] = (gate / (1.0 + jnp.exp(-gate)) * up).astype(bf16)

    total = parts_ref[0, : mine + zs].astype(f32)
    for n in range(1, ns):
        total = total + parts_ref[n, : mine + zs].astype(f32)
    own, centre, scale = norm(where_ref[0] * mine, mine)
    query = total[:mine] + shift(own, centre, 3, lambda to: (to & 7) >= 6, tails)
    query = (query * jnp.concatenate([scale] * (cols // 128), axis=1)).astype(bf16)
    start = iota((mine, zs), 1) * toks
    at = iota((mine, zs), 0)
    expand = jnp.where((at >= start) & (at < start + toks), 1.0, 0.0).astype(bf16)
    pairs = jnp.zeros((mine, half), f32)
    for part in parts_of(total[mine:, :half], 3):
        pairs = pairs + jnp.dot(expand, part.astype(bf16), preferred_element_type=f32)
    pair_cols = 2 * cols // zs // 2
    at = iota((128, half), 1)
    spread = jnp.where((lax.rem(at, pair_cols) == iota((128, half), 0)) & (at < toks * pair_cols), 1.0, 0.0)
    shifted = shift(own, centre, 3, lambda to: (to & 7) < 2, tails[:, every:])
    for part in parts_of(shifted, 3):
        pairs = pairs + jnp.dot(part.astype(bf16), spread.astype(bf16), preferred_element_type=f32)
    pairs = pairs * jnp.concatenate([scale] * (half // 128), axis=1)
    start = lax.rem(iota((mine, half), 0), toks) * pair_cols
    at = iota((mine, half), 1)
    pairs = jnp.where((at >= start) & (at < start + pair_cols), pairs, 0.0).astype(bf16)
    shape = (zs * 8, mine)
    to, at = iota(shape, 0), iota(shape, 1)
    row = to & 7
    start = lax.shift_right_logical(to, 3) * toks
    take = jnp.where((row < toks) & (at == start + row), 1.0, 0.0).astype(bf16)
    block_ref[...] = jnp.dot(take, query, preferred_element_type=f32).astype(bf16)
    take = jnp.where((row == toks) & (at >= start) & (at < start + toks), 1.0, 0.0).astype(bf16)
    pairs = jnp.dot(take, pairs, preferred_element_type=f32)
    block_ref[:, :half] = (block_ref[:, :half].astype(f32) + pairs).astype(bf16)


def last_kernel(toks, per_z, parts_ref, source_ref, down_source_ref, mixed_ref, weights_ref, down_ref, sems):
    ns, rows, cols = parts_ref.shape
    mine = mixed_ref.shape[0]
    zs = rows - mine
    copies = [
        pltpu.make_async_copy(source_ref, weights_ref, sems.at[0]),
        pltpu.make_async_copy(down_source_ref, down_ref, sems.at[1]),
    ]
    for copy in copies:
        copy.start()
    head = cols // per_z
    shape = (ns * mine, ns * zs)
    start = iota(shape, 1) * toks
    at = iota(shape, 0)
    expand = jnp.where((at >= start) & (at < start + toks), 1.0, 0.0).astype(bf16)
    shape = (ns * mine, 128)
    at = iota(shape, 1)
    own = (lax.rem(at, 8) == lax.rem(iota(shape, 0), toks)) & (at < 48)
    at = iota((128, 128), 0)
    pick_top = jnp.where(at < 24, 1.0, 0.0).astype(bf16)
    pick_total = jnp.where((at >= 24) & (at < 48), 1.0, 0.0).astype(bf16)
    mixed = None
    for k in range(per_z):
        marks = jnp.concatenate([parts_ref[n, mine:, k * head : k * head + 128] for n in range(ns)], axis=0)
        marks = jnp.dot(expand, marks, preferred_element_type=f32)
        marks = jnp.where(own, marks, 0.0).astype(bf16)
        tops = jnp.dot(marks, pick_top, preferred_element_type=f32)
        totals = jnp.dot(marks, pick_total, preferred_element_type=f32)
        tops = [tops[n * mine : (n + 1) * mine] for n in range(ns)]
        top = tops[0]
        for n in range(1, ns):
            top = jnp.maximum(top, tops[n])
        total = jnp.zeros((mine, 128), f32)
        weighted = jnp.zeros((mine, head), f32)
        for n in range(ns):
            scale = jnp.exp(tops[n] - top)
            total = total + totals[n * mine : (n + 1) * mine] * scale
            scale = jnp.concatenate([scale] * (head // 128), axis=1)
            weighted = weighted + parts_ref[n, :mine, k * head : (k + 1) * head].astype(f32) * scale
        total = jnp.concatenate([total] * (head // 128), axis=1)
        attended = (weighted / total).astype(bf16)
        if mixed is None:
            for copy in copies:
                copy.wait()
            mixed = down_ref[...].astype(f32)
        mixed = mixed + jnp.dot(
            attended, weights_ref[k * head : (k + 1) * head], preferred_element_type=f32
        )
    mixed_ref[...] = mixed.astype(bf16)


def local(
    activations,
    norm_gain,
    w_query,
    w_keyval,
    w_out,
    w_gate,
    w_up,
    w_down,
    key_cache,
    value_cache,
    lengths,
):
    zs, ys, ns = lax.axis_size("z"), lax.axis_size("y"), lax.axis_size(NARROW)
    ws = zs * ys
    rows, new, width = activations.shape
    toks = rows * new
    mine = zs * toks
    head_dim = key_cache.shape[2]
    kv_cols = w_keyval.shape[1]
    lanes = w_query.shape[1]
    heads = ws * lanes // head_dim
    cols = ys * lanes
    pair_cols = ys * kv_cols
    per_z = cols // head_dim
    ffn = w_gate.shape[1]

    values = activations.reshape(toks, width).astype(f32)
    gain = norm_gain.reshape(1, width)

    chunks = width // lanes
    pair_lanes = w_keyval.T.reshape(kv_cols, chunks, lanes).transpose(1, 0, 2).reshape(chunks * kv_cols, lanes)
    w_first = lax.all_gather(jnp.concatenate([w_query, pair_lanes], axis=0), "y", axis=0, tiled=False)
    w_last = lax.all_gather(w_out, "y", axis=0, tiled=True)

    packed = activations.reshape(toks * width // 128, 128)
    copies = jnp.broadcast_to(packed[None], (zs,) + packed.shape)
    column = lax.all_to_all(copies, "z", 0, 0, tiled=True).reshape(mine, width)

    flat = lax.all_gather(column, "y", axis=0, tiled=True)
    sums, notes = pl.pallas_call(
        hidden_kernel,
        out_shape=(
            jax.ShapeDtypeStruct((ys * mine, 2 * ffn), bf16),
            jax.ShapeDtypeStruct((8, 2 * ffn), f32),
        ),
        in_specs=[vmem] * 4,
        out_specs=(vmem, vmem),
        compiler_params=pltpu.CompilerParams(vmem_limit_bytes=40 * 2**20),
        cost_estimate=pl.CostEstimate(flops=2**30, bytes_accessed=4 * 2**20, transcendentals=0),
        name="hidden",
    )(flat, gain, w_gate, w_up)
    sums = lax.all_to_all(sums.reshape(ns, -1, 2 * ffn), NARROW, 0, 0, tiled=True)

    parts = pl.pallas_call(
        functools.partial(first_kernel, toks),
        out_shape=jax.ShapeDtypeStruct((mine + zs + 8, cols), bf16),
        in_specs=[vmem, vmem, vmem, hbm],
        out_specs=vmem,
        scratch_shapes=[pltpu.VMEM(w_first.shape, bf16), pltpu.SemaphoreType.DMA((ys,))],
        compiler_params=pltpu.CompilerParams(vmem_limit_bytes=24 * 2**20),
        cost_estimate=pl.CostEstimate(flops=2 * mine * width * cols, bytes_accessed=2 * 2**20, transcendentals=0),
        name="first",
    )(column, gain, notes, w_first)
    parts = lax.all_gather(parts, NARROW, axis=0, tiled=False)
    hidden, block = pl.pallas_call(
        functools.partial(second_kernel, toks),
        out_shape=(
            jax.ShapeDtypeStruct((sums.shape[1], ffn), bf16),
            jax.ShapeDtypeStruct((zs * 8, cols), bf16),
        ),
        in_specs=[smem, vmem, vmem],
        out_specs=(vmem, vmem),
        compiler_params=pltpu.CompilerParams(vmem_limit_bytes=24 * 2**20),
        cost_estimate=pl.CostEstimate(flops=2**24, bytes_accessed=2 * 2**20, transcendentals=0),
        name="second",
    )(jnp.stack([lax.axis_index("y"), lax.axis_index(NARROW)]).astype(jnp.int32), sums, parts)
    block = lax.all_to_all(block.reshape(zs, 8, cols), "z", 0, 0, tiled=True)

    queries = (
        block[:, :toks]
        .reshape(zs, rows, new, per_z, head_dim)
        .transpose(1, 2, 0, 3, 4)
        .reshape(rows, new * heads, head_dim)
    )
    pairs = (
        block[:, toks, : toks * pair_cols]
        .reshape(zs, toks, pair_cols)
        .transpose(1, 0, 2)
        .reshape(rows, new, 2 * head_dim)
    )
    new_keys, new_values = pairs[..., :head_dim], pairs[..., head_dim:]
    narrow_index = lax.axis_index(NARROW)
    cache_part = key_cache.shape[1]
    factor = head_dim ** (-0.5)
    positions = narrow_index * cache_part + jnp.arange(cache_part, dtype=jnp.int32)
    usable = (positions[None, :] < lengths[:, None])[:, None, :]
    scores = jnp.einsum("rqd,rpd->rqp", queries, key_cache, preferred_element_type=f32) * factor
    scores = jnp.where(usable, scores, masked_score)
    own = jnp.einsum("rqd,rud->rqu", queries, new_keys, preferred_element_type=f32) * factor
    token_of = np.arange(new * heads) // heads
    causal = (token_of[:, None] >= np.arange(new)[None, :])[None]
    causal = jnp.logical_and(causal, narrow_index == 0)
    own = jnp.where(causal, own, masked_score)
    top = jnp.maximum(scores.max(-1), own.max(-1))
    weights = jnp.where(usable, jnp.exp(scores - top[..., None]), 0.0)
    own_weights = jnp.where(causal, jnp.exp(own - top[..., None]), 0.0)
    total = weights.sum(-1) + own_weights.sum(-1)
    weighted = jnp.einsum("rqp,rpd->rqd", weights.astype(bf16), value_cache, preferred_element_type=f32)
    weighted = weighted + jnp.einsum("rqu,rud->rqd", own_weights, new_values.astype(f32))

    sent = (
        weighted.astype(bf16)
        .reshape(rows, new, zs, per_z, head_dim)
        .transpose(2, 0, 1, 3, 4)
        .reshape(zs, toks, cols)
    )
    marks = jnp.stack(three_parts(top) + three_parts(total)).astype(bf16)
    marks = marks.reshape(6, toks, zs, per_z).transpose(2, 3, 0, 1)
    marks = jnp.pad(marks, ((0, 0), (0, 0), (0, 0), (0, 8 - toks))).reshape(zs, per_z, 48)
    marks = jnp.pad(marks, ((0, 0), (0, 0), (0, head_dim - 48))).reshape(zs, 1, cols)
    block = jnp.concatenate([sent, marks, jnp.zeros((zs, 8 - toks - 1, cols), bf16)], axis=1)
    block = lax.all_to_all(block, "z", 0, 0, tiled=True)
    parts = jnp.concatenate([block[:, :toks].reshape(mine, cols), block[:, toks]], axis=0)
    parts = lax.all_gather(parts, NARROW, axis=0, tiled=False)
    hidden = lax.all_gather(hidden, NARROW, axis=0, tiled=True)
    down = jnp.dot(hidden, w_down, preferred_element_type=f32).astype(bf16)
    down = lax.psum_scatter(down, "y", scatter_dimension=0, tiled=True)

    mixed = pl.pallas_call(
        functools.partial(last_kernel, toks, per_z),
        out_shape=jax.ShapeDtypeStruct((mine, width), bf16),
        in_specs=[vmem, hbm, hbm],
        out_specs=vmem,
        scratch_shapes=[
            pltpu.VMEM(w_last.shape, bf16),
            pltpu.VMEM((mine, width), bf16),
            pltpu.SemaphoreType.DMA((2,)),
        ],
        compiler_params=pltpu.CompilerParams(vmem_limit_bytes=24 * 2**20),
        cost_estimate=pl.CostEstimate(
            flops=2 * mine * width * cols, bytes_accessed=3 * 2**20, transcendentals=0
        ),
        name="last",
    )(parts, w_last, down)
    mixed = mixed.reshape(zs, toks * width // 128, 128)
    mixed = lax.all_to_all(mixed, "z", 0, 0, tiled=True)
    mixed = mixed.astype(f32).sum(0).reshape(toks, width)
    return (values + mixed).astype(bf16).reshape(activations.shape)


def solution(mesh):
    names = ("z", "y", "x", "core")
    split = Mesh(mesh.devices.reshape(16, 4, 4, 2), names)
    return jax.shard_map(
        local,
        mesh=split,
        in_specs=(
            P(WIDE, None, NARROW),
            P(NARROW),
            P(NARROW, WIDE),
            P(NARROW, WIDE),
            P(WIDE, NARROW),
            P(NARROW, WIDE),
            P(NARROW, WIDE),
            P(WIDE, NARROW),
            P(WIDE, NARROW, None),
            P(WIDE, NARROW, None),
            P(WIDE),
        ),
        out_specs=P(WIDE, None, NARROW),
        check_vma=False,
    )
```

```python
import functools

import jax
import jax.numpy as jnp
import numpy as np
from jax import lax
from jax.experimental import pallas as pl
from jax.experimental.pallas import tpu as pltpu
from jax.sharding import Mesh
from jax.sharding import PartitionSpec as P

D = 8192
eps_norm = 1e-05
masked_score = -1e30
bf16 = jnp.bfloat16
f32 = jnp.float32
vmem = pl.BlockSpec(memory_space=pltpu.VMEM)
WIDE = ("z", "y")
NARROW = ("x", "core")


def three_parts(value):
    first = lax.reduce_precision(value, 8, 7)
    rest = value - first
    second = lax.reduce_precision(rest, 8, 7)
    return first, second, lax.reduce_precision(rest - second, 8, 7)


def iota(shape, axis):
    return lax.broadcasted_iota(jnp.int32, shape, axis)


def spread_kernel(packed_ref, pairs_ref, copies_ref, rows_ref):
    del pairs_ref
    ys, mine, width = copies_ref.shape
    chunks = width // 128
    rows_ref[...] = packed_ref[...].astype(f32)
    for j in range(chunks):
        chunk = rows_ref[pl.ds(j, mine, stride=chunks), :].astype(bf16)
        for y in range(ys):
            copies_ref[y, :, j * 128 : (j + 1) * 128] = chunk


def parts_of(value, count):
    found = []
    for _ in range(count):
        found.append(value.astype(bf16).astype(f32))
        value = value - found[-1]
    return found


def gain_rows(gain_ref):
    shape = (8, gain_ref.shape[1])
    rows = jnp.zeros(shape, f32)
    for k, part in enumerate(parts_of(gain_ref[...], 3)):
        rows = jnp.where(iota(shape, 0) == k, part, rows)
    return rows.astype(bf16)


def centred(tokens, gain_ref):
    tokens = tokens.astype(f32)
    total = tokens.sum(1, keepdims=True)
    mean = total * (1.0 / tokens.shape[1])
    squares = (tokens * tokens).sum(1, keepdims=True)
    return ((tokens - mean) * gain_ref[...]).astype(bf16), mean, total, squares


def across(left, right):
    return lax.dot_general(left, right, (((1,), (1,)), ((), ())), preferred_element_type=f32)


def gains_kernel(gain_ref, gate_ref, up_ref, products_ref):
    ffn = gate_ref.shape[1]
    gains = gain_rows(gain_ref)
    for k, ref in enumerate((gate_ref, up_ref)):
        product = jnp.dot(gains, ref[...], preferred_element_type=f32).sum(0, keepdims=True)
        products_ref[:, k * ffn : (k + 1) * ffn] = jnp.broadcast_to(product, (8, ffn))


def hidden_kernel(tokens_ref, gain_ref, products_ref, gate_ref, up_ref, parts_ref, sums_ref):
    ffn = gate_ref.shape[1]
    del parts_ref
    ready, mean, total, squares = centred(tokens_ref[...], gain_ref)
    for k, ref in enumerate((gate_ref, up_ref)):
        at = slice(k * ffn, (k + 1) * ffn)
        sums_ref[:, at] = jnp.dot(ready, ref[...], preferred_element_type=f32) + mean * products_ref[0:1, at]
    lane = iota((ready.shape[0], 128), 1)
    sums_ref[:, 2 * ffn :] = jnp.where(lane == 0, total, jnp.where(lane == 1, squares, 0.0))


def first_kernel(toks, column_ref, gain_ref, notes_ref, weights_ref, pairs_ref, parts_ref):
    ys, mine, width = column_ref.shape
    lanes = weights_ref.shape[2]
    cols = ys * lanes
    half = cols // 2
    zs = mine // toks
    chunks = width // lanes
    column, _, total, squares = centred(column_ref[0], gain_ref)
    gains = gain_rows(gain_ref)
    pairs, products = [], []
    for k in range(ys):
        query = jnp.dot(column, weights_ref[k], preferred_element_type=f32)
        parts_ref[:mine, k * lanes : (k + 1) * lanes] = query.astype(bf16)
        products.append(jnp.dot(gains, weights_ref[k], preferred_element_type=f32))
        rows = pairs_ref[k].astype(f32)
        count = rows.shape[0] // chunks
        pairs.append(jnp.concatenate([rows[j * count : (j + 1) * count] for j in range(chunks)], axis=1))
    pairs = jnp.concatenate(pairs, axis=0)
    count = pairs.shape[0]
    pairs = jnp.concatenate([pairs, jnp.zeros((128 - count, width), f32)], axis=0).astype(bf16)
    pair_products = across(gains, pairs).sum(0, keepdims=True)
    pairs = across(column, pairs).astype(bf16)
    at = iota((128, half), 1)
    spread = jnp.where((lax.rem(at, count) == iota((128, half), 0)) & (at < toks * count), 1.0, 0.0)
    pairs = jnp.dot(pairs, spread.astype(bf16), preferred_element_type=f32)
    start = lax.rem(iota((mine, half), 0), toks) * count
    at = iota((mine, half), 1)
    pairs = jnp.where((at >= start) & (at < start + count), pairs, 0.0).astype(bf16)
    start = iota((zs, mine), 0) * toks
    at = iota((zs, mine), 1)
    collect = jnp.where((at >= start) & (at < start + toks), 1.0, 0.0).astype(bf16)
    pairs = jnp.dot(collect, pairs, preferred_element_type=f32)

    row = iota((zs, half), 0)
    beside = jnp.zeros((zs, half), f32)
    for j in range(4):
        high, low = parts_of(notes_ref[0:1, j * half : (j + 1) * half], 2)
        beside = jnp.where(row == j, high, jnp.where(row == 4 + j, low, beside))
    parts_ref[mine : mine + zs] = jnp.concatenate([pairs, beside], axis=1).astype(bf16)

    row = iota((8, cols), 0)
    tail = jnp.zeros((8, cols), f32)
    for k, value in enumerate((total, squares)):
        value = jnp.concatenate([jnp.broadcast_to(value, (mine, 128)), jnp.zeros((128 - mine, 128), f32)], axis=0)
        value = jnp.concatenate([value.T[0:1], jnp.zeros((1, cols - 128), f32)], axis=1)
        for j, part in enumerate(parts_of(value, 3)):
            tail = jnp.where(row == 3 * k + j, part, tail)
    products = jnp.concatenate(products, axis=1).sum(0, keepdims=True)
    for k, part in enumerate(parts_of(products, 2)):
        tail = jnp.where(row == 6 + k, part, tail)
    pair_products = jnp.concatenate([jnp.zeros((1, cols - 128), f32), pair_products], axis=1)
    for k, part in enumerate(parts_of(pair_products, 2)):
        tail = jnp.where((row == k) & (iota((8, cols), 1) >= cols - 128), part, tail)
    parts_ref[mine + zs :] = tail.astype(bf16)


def pick(shape, group, mask):
    frm, to = iota(shape, 0), iota(shape, 1)
    kind = frm & 7
    same = lax.shift_right_logical(frm, 3) == lax.shift_right_logical(to, group)
    return jnp.where(same & (kind < 3) & mask(to), 1.0, 0.0).astype(bf16)


def norm(tails, first, count):
    every = tails.shape[1] - 128
    shape = (count, every)
    select = jnp.where(iota(shape, 1) == iota(shape, 0) + first, 1.0, 0.0).astype(bf16)
    own = across(select, tails[:, :every]).astype(bf16)
    kind = iota((tails.shape[0], 128), 0) & 7
    total = jnp.dot(own, jnp.where(kind < 3, 1.0, 0.0).astype(bf16), preferred_element_type=f32)
    centre = total * (1.0 / D)
    total = jnp.dot(
        own, jnp.where((kind >= 3) & (kind < 6), 1.0, 0.0).astype(bf16), preferred_element_type=f32
    )
    spread = total * (1.0 / D) - centre * centre
    return own, centre, lax.rsqrt(spread + eps_norm)


def shift(own, centre, group, mask, table, width):
    shape = (own.shape[1], table.shape[0])
    means = jnp.dot(own, pick(shape, group, mask), preferred_element_type=f32) * (1.0 / width)
    shape = (own.shape[0], table.shape[0])
    means = jnp.where(mask(iota(shape, 1)), means - centre[:, : shape[1]], 0.0)
    high, low = parts_of(means, 2)
    return jnp.dot(high.astype(bf16), table, preferred_element_type=f32) + jnp.dot(
        low.astype(bf16), table, preferred_element_type=f32
    )


def tails_of(parts_ref, first):
    ns = parts_ref.shape[0]
    return jnp.concatenate([parts_ref[n, first:].astype(f32) for n in range(ns)], axis=0).astype(bf16)


def third_kernel(toks, sums_ref, parts_ref, hidden_ref):
    ns, rows, cols = parts_ref.shape
    ffn = hidden_ref.shape[1]
    half = cols // 2
    zs = (rows - 8) // (toks + 1)
    mine = zs * toks
    besides = jnp.concatenate([parts_ref[n, mine : mine + zs, half:] for n in range(ns)], axis=0)
    at = iota((8, ns * zs), 1) & (zs - 1)
    centre = sums_ref[:, 2 * ffn : 2 * ffn + 1] * (1.0 / D)
    spread = sums_ref[:, 2 * ffn + 1 : 2 * ffn + 2] * (1.0 / D) - centre * centre
    scale = lax.rsqrt(spread + eps_norm)
    for j in range(2):
        both = []
        for k in (j, j + 2):
            take = jnp.where((at == k) | (at == k + 4), 1.0, 0.0).astype(bf16)
            product = jnp.dot(take, besides, preferred_element_type=f32)[0:1]
            both.append((sums_ref[:, k * half : (k + 1) * half] - centre * product) * scale)
        gate, up = both
        hidden_ref[:, j * half : (j + 1) * half] = (gate / (1.0 + jnp.exp(-gate)) * up).astype(bf16)


def second_kernel(toks, width, parts_ref, block_ref):
    ns, rows, cols = parts_ref.shape
    half = cols // 2
    zs = block_ref.shape[0] // 8
    mine = zs * toks
    every = cols - 128
    tails = tails_of(parts_ref, mine + zs)
    total = parts_ref[0, : mine + zs].astype(f32)
    for n in range(1, ns):
        total = total + parts_ref[n, : mine + zs].astype(f32)
    own, centre, scale = norm(tails, 0, mine)
    query = total[:mine] + shift(own, centre, 3, lambda to: (to & 7) >= 6, tails, width)
    query = (query * jnp.concatenate([scale] * (cols // 128), axis=1)).astype(bf16)
    start = iota((mine, zs), 1) * toks
    at = iota((mine, zs), 0)
    expand = jnp.where((at >= start) & (at < start + toks), 1.0, 0.0).astype(bf16)
    pairs = jnp.zeros((mine, half), f32)
    for part in parts_of(total[mine:, :half], 3):
        pairs = pairs + jnp.dot(expand, part.astype(bf16), preferred_element_type=f32)
    pair_cols = 2 * cols // zs // 2
    at = iota((128, half), 1)
    spread = jnp.where((lax.rem(at, pair_cols) == iota((128, half), 0)) & (at < toks * pair_cols), 1.0, 0.0)
    shifted = shift(own, centre, 3, lambda to: (to & 7) < 2, tails[:, every:], width)
    for part in parts_of(shifted, 3):
        pairs = pairs + jnp.dot(part.astype(bf16), spread.astype(bf16), preferred_element_type=f32)
    pairs = pairs * jnp.concatenate([scale] * (half // 128), axis=1)
    start = lax.rem(iota((mine, half), 0), toks) * pair_cols
    at = iota((mine, half), 1)
    pairs = jnp.where((at >= start) & (at < start + pair_cols), pairs, 0.0).astype(bf16)
    shape = (zs * 8, mine)
    to, at = iota(shape, 0), iota(shape, 1)
    row = to & 7
    start = lax.shift_right_logical(to, 3) * toks
    take = jnp.where((row < toks) & (at == start + row), 1.0, 0.0).astype(bf16)
    block_ref[...] = jnp.dot(take, query, preferred_element_type=f32).astype(bf16)
    take = jnp.where((row == toks) & (at >= start) & (at < start + toks), 1.0, 0.0).astype(bf16)
    pairs = jnp.dot(take, pairs, preferred_element_type=f32)
    block_ref[:, :half] = (block_ref[:, :half].astype(f32) + pairs).astype(bf16)


def last_kernel(toks, per_z, parts_ref, weights_ref, down_ref, mixed_ref):
    ns, rows, cols = parts_ref.shape
    mine = mixed_ref.shape[0]
    zs = rows - mine
    head = cols // per_z
    shape = (ns * mine, ns * zs)
    start = iota(shape, 1) * toks
    at = iota(shape, 0)
    expand = jnp.where((at >= start) & (at < start + toks), 1.0, 0.0).astype(bf16)
    shape = (ns * mine, 128)
    at = iota(shape, 1)
    own = (lax.rem(at, 8) == lax.rem(iota(shape, 0), toks)) & (at < 48)
    at = iota((128, 128), 0)
    pick_top = jnp.where(at < 24, 1.0, 0.0).astype(bf16)
    pick_total = jnp.where((at >= 24) & (at < 48), 1.0, 0.0).astype(bf16)
    mixed = down_ref[0].astype(f32)
    for k in range(1, down_ref.shape[0]):
        mixed = mixed + down_ref[k].astype(f32)
    for k in range(per_z):
        marks = jnp.concatenate([parts_ref[n, mine:, k * head : k * head + 128] for n in range(ns)], axis=0)
        marks = jnp.dot(expand, marks, preferred_element_type=f32)
        marks = jnp.where(own, marks, 0.0).astype(bf16)
        tops = jnp.dot(marks, pick_top, preferred_element_type=f32)
        totals = jnp.dot(marks, pick_total, preferred_element_type=f32)
        tops = [tops[n * mine : (n + 1) * mine] for n in range(ns)]
        top = tops[0]
        for n in range(1, ns):
            top = jnp.maximum(top, tops[n])
        total = jnp.zeros((mine, 128), f32)
        weighted = jnp.zeros((mine, head), f32)
        for n in range(ns):
            scale = jnp.exp(tops[n] - top)
            total = total + totals[n * mine : (n + 1) * mine] * scale
            scale = jnp.concatenate([scale] * (head // 128), axis=1)
            weighted = weighted + parts_ref[n, :mine, k * head : (k + 1) * head].astype(f32) * scale
        total = jnp.concatenate([total] * (head // 128), axis=1)
        attended = (weighted / total).astype(bf16)
        mixed = mixed + jnp.dot(
            attended, weights_ref[k * head : (k + 1) * head], preferred_element_type=f32
        )
    mixed_ref[...] = mixed.astype(bf16)


def local(
    activations,
    norm_gain,
    w_query,
    w_keyval,
    w_out,
    w_gate,
    w_up,
    w_down,
    key_cache,
    value_cache,
    lengths,
):
    zs, ys, ns = lax.axis_size("z"), lax.axis_size("y"), lax.axis_size(NARROW)
    ws = zs * ys
    rows, new, width = activations.shape
    toks = rows * new
    mine = zs * toks
    head_dim = key_cache.shape[2]
    kv_cols = w_keyval.shape[1]
    lanes = w_query.shape[1]
    heads = ws * lanes // head_dim
    cols = ys * lanes
    pair_cols = ys * kv_cols
    per_z = cols // head_dim
    ffn = w_gate.shape[1]

    values = activations.reshape(toks, width).astype(f32)
    gain = norm_gain.reshape(1, width)

    chunks = width // lanes
    pair_lanes = w_keyval.T.reshape(kv_cols, chunks, lanes).transpose(1, 0, 2).reshape(chunks * kv_cols, lanes)
    w_first = lax.all_gather(w_query, "y", axis=0, tiled=False)
    w_pair = lax.all_gather(pair_lanes, "y", axis=0, tiled=False)
    w_last = lax.all_gather(w_out, "y", axis=0, tiled=True)

    packed = activations.reshape(toks * width // 128, 128)
    copies = jnp.broadcast_to(packed[None], (zs,) + packed.shape)
    column = lax.all_to_all(copies, "z", 0, 0, tiled=True)
    column = pl.pallas_call(
        spread_kernel,
        out_shape=jax.ShapeDtypeStruct((ys, mine, width), bf16),
        in_specs=[vmem, vmem],
        out_specs=vmem,
        scratch_shapes=[pltpu.VMEM((mine * width // 128, 128), f32)],
        compiler_params=pltpu.CompilerParams(vmem_limit_bytes=8 * 2**20),
        cost_estimate=pl.CostEstimate(flops=0, bytes_accessed=2**20, transcendentals=0),
        name="spread",
    )(column.reshape(mine * width // 128, 128), w_pair)

    products = pl.pallas_call(
        gains_kernel,
        out_shape=jax.ShapeDtypeStruct((8, 2 * ffn), f32),
        in_specs=[vmem] * 3,
        out_specs=vmem,
        compiler_params=pltpu.CompilerParams(vmem_limit_bytes=8 * 2**20),
        cost_estimate=pl.CostEstimate(flops=2**25, bytes_accessed=2 * 2**20, transcendentals=0),
        name="gains",
    )(gain, w_gate, w_up)
    flat = lax.all_to_all(column, "y", 0, 0, tiled=True).reshape(ys * mine, width)
    parts = pl.pallas_call(
        functools.partial(first_kernel, toks),
        out_shape=jax.ShapeDtypeStruct((mine + zs + 8, cols), bf16),
        in_specs=[vmem] * 5,
        out_specs=vmem,
        compiler_params=pltpu.CompilerParams(vmem_limit_bytes=12 * 2**20),
        cost_estimate=pl.CostEstimate(flops=2 * mine * width * cols, bytes_accessed=2 * 2**20, transcendentals=0),
        name="first",
    )(column, gain, products, w_first, w_pair)

    sums = pl.pallas_call(
        hidden_kernel,
        out_shape=jax.ShapeDtypeStruct((ys * mine, 2 * ffn + 128), f32),
        in_specs=[vmem] * 6,
        out_specs=vmem,
        compiler_params=pltpu.CompilerParams(vmem_limit_bytes=16 * 2**20),
        cost_estimate=pl.CostEstimate(flops=2**30, bytes_accessed=4 * 2**20, transcendentals=0),
        name="hidden",
    )(flat, gain, products, w_gate, w_up, parts)
    sums = lax.psum_scatter(sums, NARROW, scatter_dimension=0, tiled=True)

    parts = lax.all_gather(parts, NARROW, axis=0, tiled=False)
    notes = parts
    block = pl.pallas_call(
        functools.partial(second_kernel, toks, width),
        out_shape=jax.ShapeDtypeStruct((zs * 8, cols), bf16),
        in_specs=[vmem],
        out_specs=vmem,
        compiler_params=pltpu.CompilerParams(vmem_limit_bytes=12 * 2**20),
        cost_estimate=pl.CostEstimate(flops=2**24, bytes_accessed=2 * 2**20, transcendentals=0),
        name="second",
    )(parts)
    block = lax.all_to_all(block.reshape(zs, 8, cols), "z", 0, 0, tiled=True)

    queries = (
        block[:, :toks]
        .reshape(zs, rows, new, per_z, head_dim)
        .transpose(1, 2, 0, 3, 4)
        .reshape(rows, new * heads, head_dim)
    )
    pairs = (
        block[:, toks, : toks * pair_cols]
        .reshape(zs, toks, pair_cols)
        .transpose(1, 0, 2)
        .reshape(rows, new, 2 * head_dim)
    )
    new_keys, new_values = pairs[..., :head_dim], pairs[..., head_dim:]
    narrow_index = lax.axis_index(NARROW)
    cache_part = key_cache.shape[1]
    factor = head_dim ** (-0.5)
    positions = narrow_index * cache_part + jnp.arange(cache_part, dtype=jnp.int32)
    usable = (positions[None, :] < lengths[:, None])[:, None, :]
    scores = jnp.einsum("rqd,rpd->rqp", queries, key_cache, preferred_element_type=f32) * factor
    scores = jnp.where(usable, scores, masked_score)
    own = jnp.einsum("rqd,rud->rqu", queries, new_keys, preferred_element_type=f32) * factor
    token_of = np.arange(new * heads) // heads
    causal = (token_of[:, None] >= np.arange(new)[None, :])[None]
    causal = jnp.logical_and(causal, narrow_index == 0)
    own = jnp.where(causal, own, masked_score)
    top = jnp.maximum(scores.max(-1), own.max(-1))
    weights = jnp.where(usable, jnp.exp(scores - top[..., None]), 0.0)
    own_weights = jnp.where(causal, jnp.exp(own - top[..., None]), 0.0)
    total = weights.sum(-1) + own_weights.sum(-1)
    weighted = jnp.einsum("rqp,rpd->rqd", weights.astype(bf16), value_cache, preferred_element_type=f32)
    weighted = weighted + jnp.einsum("rqu,rud->rqd", own_weights, new_values.astype(f32))

    sent = (
        weighted.astype(bf16)
        .reshape(rows, new, zs, per_z, head_dim)
        .transpose(2, 0, 1, 3, 4)
        .reshape(zs, toks, cols)
    )
    marks = jnp.stack(three_parts(top) + three_parts(total)).astype(bf16)
    marks = marks.reshape(6, toks, zs, per_z).transpose(2, 3, 0, 1)
    marks = jnp.pad(marks, ((0, 0), (0, 0), (0, 0), (0, 8 - toks))).reshape(zs, per_z, 48)
    marks = jnp.pad(marks, ((0, 0), (0, 0), (0, head_dim - 48))).reshape(zs, 1, cols)
    block = jnp.concatenate([sent, marks, jnp.zeros((zs, 8 - toks - 1, cols), bf16)], axis=1)
    block = lax.all_to_all(block, "z", 0, 0, tiled=True)
    parts = jnp.concatenate([block[:, :toks].reshape(mine, cols), block[:, toks]], axis=0)
    parts = lax.all_gather(parts, NARROW, axis=0, tiled=False)
    hidden = pl.pallas_call(
        functools.partial(third_kernel, toks),
        out_shape=jax.ShapeDtypeStruct((sums.shape[0], ffn), bf16),
        in_specs=[vmem, vmem],
        out_specs=vmem,
        compiler_params=pltpu.CompilerParams(vmem_limit_bytes=8 * 2**20),
        cost_estimate=pl.CostEstimate(flops=2**24, bytes_accessed=2 * 2**20, transcendentals=0),
        name="third",
    )(sums, notes)
    hidden = lax.all_gather(hidden, NARROW, axis=0, tiled=True)
    down = jnp.dot(hidden, w_down, preferred_element_type=f32).astype(bf16)
    down = lax.all_to_all(down.reshape(ys, mine, width), "y", 0, 0, tiled=True)

    mixed = pl.pallas_call(
        functools.partial(last_kernel, toks, per_z),
        out_shape=jax.ShapeDtypeStruct((mine, width), bf16),
        in_specs=[vmem, vmem, vmem],
        out_specs=vmem,
        compiler_params=pltpu.CompilerParams(vmem_limit_bytes=12 * 2**20),
        cost_estimate=pl.CostEstimate(
            flops=2 * mine * width * cols, bytes_accessed=3 * 2**20, transcendentals=0
        ),
        name="last",
    )(parts, w_last, down)
    mixed = mixed.reshape(zs, toks * width // 128, 128)
    mixed = lax.all_to_all(mixed, "z", 0, 0, tiled=True)
    mixed = mixed.astype(f32).sum(0).reshape(toks, width)
    return (values + mixed).astype(bf16).reshape(activations.shape)


def solution(mesh):
    names = ("z", "y", "x", "core")
    split = Mesh(mesh.devices.reshape(16, 4, 4, 2), names)
    return jax.shard_map(
        local,
        mesh=split,
        in_specs=(
            P(WIDE, None, NARROW),
            P(NARROW),
            P(NARROW, WIDE),
            P(NARROW, WIDE),
            P(WIDE, NARROW),
            P(NARROW, WIDE),
            P(NARROW, WIDE),
            P(WIDE, NARROW),
            P(WIDE, NARROW, None),
            P(WIDE, NARROW, None),
            P(WIDE),
        ),
        out_specs=P(WIDE, None, NARROW),
        check_vma=False,
    )
```

```python
import functools

import jax
import jax.numpy as jnp
import numpy as np
from jax import lax
from jax.experimental import pallas as pl
from jax.experimental.pallas import tpu as pltpu
from jax.sharding import Mesh
from jax.sharding import PartitionSpec as P

D = 8192
eps_norm = 1e-05
masked_score = -1e30
bf16 = jnp.bfloat16
f32 = jnp.float32
vmem = pl.BlockSpec(memory_space=pltpu.VMEM)
anywhere = pl.BlockSpec(memory_space=pl.ANY)
WIDE = ("z", "y")
NARROW = ("x", "core")


def three_parts(value):
    first = lax.reduce_precision(value, 8, 7)
    rest = value - first
    second = lax.reduce_precision(rest, 8, 7)
    return first, second, lax.reduce_precision(rest - second, 8, 7)


def iota(shape, axis):
    return lax.broadcasted_iota(jnp.int32, shape, axis)


def spread_kernel(packed_ref, pairs_ref, copies_ref, rows_ref):
    del pairs_ref
    ys, mine, width = copies_ref.shape
    chunks = width // 128
    rows_ref[...] = packed_ref[...].astype(f32)
    for j in range(chunks):
        chunk = rows_ref[pl.ds(j, mine, stride=chunks), :].astype(bf16)
        for y in range(ys):
            copies_ref[y, :, j * 128 : (j + 1) * 128] = chunk


def parts_of(value, count):
    found = []
    for _ in range(count):
        found.append(value.astype(bf16).astype(f32))
        value = value - found[-1]
    return found


def gain_rows(gain_ref):
    shape = (8, gain_ref.shape[1])
    rows = jnp.zeros(shape, f32)
    for k, part in enumerate(parts_of(gain_ref[...], 3)):
        rows = jnp.where(iota(shape, 0) == k, part, rows)
    return rows.astype(bf16)


def centred(tokens, gain_ref):
    tokens = tokens.astype(f32)
    total = tokens.sum(1, keepdims=True)
    mean = total * (1.0 / tokens.shape[1])
    squares = (tokens * tokens).sum(1, keepdims=True)
    return ((tokens - mean) * gain_ref[...]).astype(bf16), mean, total, squares


def across(left, right):
    return lax.dot_general(left, right, (((1,), (1,)), ((), ())), preferred_element_type=f32)


def gains_kernel(gain_ref, gate_ref, up_ref, products_ref):
    ffn = gate_ref.shape[1]
    gains = gain_rows(gain_ref)
    for k, ref in enumerate((gate_ref, up_ref)):
        product = jnp.dot(gains, ref[...], preferred_element_type=f32).sum(0, keepdims=True)
        products_ref[:, k * ffn : (k + 1) * ffn] = jnp.broadcast_to(product, (8, ffn))


def hidden_kernel(
    source_ref, gain_ref, products_ref, gate_ref, up_ref, parts_ref, out_ref, tokens_ref, sums_ref, arrived, sent
):
    del parts_ref
    ffn = gate_ref.shape[1]
    pieces = arrived.shape[0]
    count = source_ref.shape[0] // pieces
    lane = iota((count, 128), 1)
    rows = [slice(j * count, (j + 1) * count) for j in range(pieces)]
    reads = [pltpu.make_async_copy(source_ref.at[at], tokens_ref.at[at], arrived.at[j]) for j, at in enumerate(rows)]
    writes = [pltpu.make_async_copy(sums_ref.at[at], out_ref.at[at], sent.at[j]) for j, at in enumerate(rows)]
    for read in reads:
        read.start()
    for j, at in enumerate(rows):
        reads[j].wait()
        ready, mean, total, squares = centred(tokens_ref[at], gain_ref)
        for k, ref in enumerate((gate_ref, up_ref)):
            product = jnp.dot(ready, ref[...], preferred_element_type=f32)
            sums_ref[at, k * ffn : (k + 1) * ffn] = product + mean * products_ref[0:1, k * ffn : (k + 1) * ffn]
        sums_ref[at, 2 * ffn :] = jnp.where(lane == 0, total, jnp.where(lane == 1, squares, 0.0))
        writes[j].start()
    for write in writes:
        write.wait()


def first_kernel(toks, column_ref, gain_ref, notes_ref, weights_ref, pairs_ref, parts_ref):
    ys, mine, width = column_ref.shape
    lanes = weights_ref.shape[2]
    cols = ys * lanes
    half = cols // 2
    zs = mine // toks
    chunks = width // lanes
    column, _, total, squares = centred(column_ref[0], gain_ref)
    gains = gain_rows(gain_ref)
    pairs, products = [], []
    for k in range(ys):
        query = jnp.dot(column, weights_ref[k], preferred_element_type=f32)
        parts_ref[:mine, k * lanes : (k + 1) * lanes] = query.astype(bf16)
        products.append(jnp.dot(gains, weights_ref[k], preferred_element_type=f32))
        rows = pairs_ref[k].astype(f32)
        count = rows.shape[0] // chunks
        pairs.append(jnp.concatenate([rows[j * count : (j + 1) * count] for j in range(chunks)], axis=1))
    pairs = jnp.concatenate(pairs, axis=0)
    count = pairs.shape[0]
    pairs = jnp.concatenate([pairs, jnp.zeros((128 - count, width), f32)], axis=0).astype(bf16)
    pair_products = across(gains, pairs).sum(0, keepdims=True)
    pairs = across(column, pairs).astype(bf16)
    at = iota((128, half), 1)
    spread = jnp.where((lax.rem(at, count) == iota((128, half), 0)) & (at < toks * count), 1.0, 0.0)
    pairs = jnp.dot(pairs, spread.astype(bf16), preferred_element_type=f32)
    start = lax.rem(iota((mine, half), 0), toks) * count
    at = iota((mine, half), 1)
    pairs = jnp.where((at >= start) & (at < start + count), pairs, 0.0).astype(bf16)
    start = iota((zs, mine), 0) * toks
    at = iota((zs, mine), 1)
    collect = jnp.where((at >= start) & (at < start + toks), 1.0, 0.0).astype(bf16)
    pairs = jnp.dot(collect, pairs, preferred_element_type=f32)

    row = iota((zs, half), 0)
    beside = jnp.zeros((zs, half), f32)
    for j in range(4):
        high, low = parts_of(notes_ref[0:1, j * half : (j + 1) * half], 2)
        beside = jnp.where(row == j, high, jnp.where(row == 4 + j, low, beside))
    parts_ref[mine : mine + zs] = jnp.concatenate([pairs, beside], axis=1).astype(bf16)

    row = iota((8, cols), 0)
    tail = jnp.zeros((8, cols), f32)
    for k, value in enumerate((total, squares)):
        value = jnp.concatenate([jnp.broadcast_to(value, (mine, 128)), jnp.zeros((128 - mine, 128), f32)], axis=0)
        value = jnp.concatenate([value.T[0:1], jnp.zeros((1, cols - 128), f32)], axis=1)
        for j, part in enumerate(parts_of(value, 3)):
            tail = jnp.where(row == 3 * k + j, part, tail)
    products = jnp.concatenate(products, axis=1).sum(0, keepdims=True)
    for k, part in enumerate(parts_of(products, 2)):
        tail = jnp.where(row == 6 + k, part, tail)
    pair_products = jnp.concatenate([jnp.zeros((1, cols - 128), f32), pair_products], axis=1)
    for k, part in enumerate(parts_of(pair_products, 2)):
        tail = jnp.where((row == k) & (iota((8, cols), 1) >= cols - 128), part, tail)
    parts_ref[mine + zs :] = tail.astype(bf16)


def pick(shape, group, mask):
    frm, to = iota(shape, 0), iota(shape, 1)
    kind = frm & 7
    same = lax.shift_right_logical(frm, 3) == lax.shift_right_logical(to, group)
    return jnp.where(same & (kind < 3) & mask(to), 1.0, 0.0).astype(bf16)


def norm(tails, first, count):
    every = tails.shape[1] - 128
    shape = (count, every)
    select = jnp.where(iota(shape, 1) == iota(shape, 0) + first, 1.0, 0.0).astype(bf16)
    own = across(select, tails[:, :every]).astype(bf16)
    kind = iota((tails.shape[0], 128), 0) & 7
    total = jnp.dot(own, jnp.where(kind < 3, 1.0, 0.0).astype(bf16), preferred_element_type=f32)
    centre = total * (1.0 / D)
    total = jnp.dot(
        own, jnp.where((kind >= 3) & (kind < 6), 1.0, 0.0).astype(bf16), preferred_element_type=f32
    )
    spread = total * (1.0 / D) - centre * centre
    return own, centre, lax.rsqrt(spread + eps_norm)


def shift(own, centre, group, mask, table, width):
    shape = (own.shape[1], table.shape[0])
    means = jnp.dot(own, pick(shape, group, mask), preferred_element_type=f32) * (1.0 / width)
    shape = (own.shape[0], table.shape[0])
    means = jnp.where(mask(iota(shape, 1)), means - centre[:, : shape[1]], 0.0)
    high, low = parts_of(means, 2)
    return jnp.dot(high.astype(bf16), table, preferred_element_type=f32) + jnp.dot(
        low.astype(bf16), table, preferred_element_type=f32
    )


def tails_of(parts_ref, first):
    ns = parts_ref.shape[0]
    return jnp.concatenate([parts_ref[n, first:].astype(f32) for n in range(ns)], axis=0).astype(bf16)


def third_kernel(toks, sums_ref, parts_ref, hidden_ref):
    ns, rows, cols = parts_ref.shape
    ffn = hidden_ref.shape[1]
    half = cols // 2
    zs = (rows - 8) // (toks + 1)
    mine = zs * toks
    besides = jnp.concatenate([parts_ref[n, mine : mine + zs, half:] for n in range(ns)], axis=0)
    at = iota((8, ns * zs), 1) & (zs - 1)
    centre = sums_ref[:, 2 * ffn : 2 * ffn + 1] * (1.0 / D)
    spread = sums_ref[:, 2 * ffn + 1 : 2 * ffn + 2] * (1.0 / D) - centre * centre
    scale = lax.rsqrt(spread + eps_norm)
    for j in range(2):
        both = []
        for k in (j, j + 2):
            take = jnp.where((at == k) | (at == k + 4), 1.0, 0.0).astype(bf16)
            product = jnp.dot(take, besides, preferred_element_type=f32)[0:1]
            both.append((sums_ref[:, k * half : (k + 1) * half] - centre * product) * scale)
        gate, up = both
        hidden_ref[:, j * half : (j + 1) * half] = (gate / (1.0 + jnp.exp(-gate)) * up).astype(bf16)


def second_kernel(toks, width, parts_ref, block_ref):
    ns, rows, cols = parts_ref.shape
    half = cols // 2
    zs = block_ref.shape[0] // 8
    mine = zs * toks
    every = cols - 128
    tails = tails_of(parts_ref, mine + zs)
    total = parts_ref[0, : mine + zs].astype(f32)
    for n in range(1, ns):
        total = total + parts_ref[n, : mine + zs].astype(f32)
    own, centre, scale = norm(tails, 0, mine)
    query = total[:mine] + shift(own, centre, 3, lambda to: (to & 7) >= 6, tails, width)
    query = (query * jnp.concatenate([scale] * (cols // 128), axis=1)).astype(bf16)
    start = iota((mine, zs), 1) * toks
    at = iota((mine, zs), 0)
    expand = jnp.where((at >= start) & (at < start + toks), 1.0, 0.0).astype(bf16)
    pairs = jnp.zeros((mine, half), f32)
    for part in parts_of(total[mine:, :half], 3):
        pairs = pairs + jnp.dot(expand, part.astype(bf16), preferred_element_type=f32)
    pair_cols = 2 * cols // zs // 2
    at = iota((128, half), 1)
    spread = jnp.where((lax.rem(at, pair_cols) == iota((128, half), 0)) & (at < toks * pair_cols), 1.0, 0.0)
    shifted = shift(own, centre, 3, lambda to: (to & 7) < 2, tails[:, every:], width)
    for part in parts_of(shifted, 3):
        pairs = pairs + jnp.dot(part.astype(bf16), spread.astype(bf16), preferred_element_type=f32)
    pairs = pairs * jnp.concatenate([scale] * (half // 128), axis=1)
    start = lax.rem(iota((mine, half), 0), toks) * pair_cols
    at = iota((mine, half), 1)
    pairs = jnp.where((at >= start) & (at < start + pair_cols), pairs, 0.0).astype(bf16)
    shape = (zs * 8, mine)
    to, at = iota(shape, 0), iota(shape, 1)
    row = to & 7
    start = lax.shift_right_logical(to, 3) * toks
    take = jnp.where((row < toks) & (at == start + row), 1.0, 0.0).astype(bf16)
    block_ref[...] = jnp.dot(take, query, preferred_element_type=f32).astype(bf16)
    take = jnp.where((row == toks) & (at >= start) & (at < start + toks), 1.0, 0.0).astype(bf16)
    pairs = jnp.dot(take, pairs, preferred_element_type=f32)
    block_ref[:, :half] = (block_ref[:, :half].astype(f32) + pairs).astype(bf16)


def attend_kernel(new, lengths_ref, block_ref, keys_ref, values_ref, sent_ref):
    rows, part, head = keys_ref.shape
    size, cols = block_ref.shape
    zs = size // 8
    toks = rows * new
    groups = cols // head
    pair_cols = 2 * head // zs
    half = cols // 2
    count = zs * new
    narrow = lax.axis_index("x") * lax.axis_size("core") + lax.axis_index("core")
    block = block_ref[...]

    def place(shape, axis, target):
        at = iota(shape, axis)
        row = lax.div(at, count)
        at = at - row * count
        z = lax.div(at, new)
        to = z * 8 + (toks if target is None else row * new + at - z * new)
        return jnp.where(iota(shape, 1 - axis) == to, 1.0, 0.0).astype(bf16)

    def by_group(values):
        return [
            jnp.concatenate([values[(r * groups + k) * count : (r * groups + k + 1) * count] for r in range(rows)], axis=0)
            for k in range(groups)
        ]

    chosen = jnp.dot(place((rows * count, size), 0, 0), block, preferred_element_type=f32).astype(bf16)
    queries = [
        jnp.concatenate([chosen[r * count : (r + 1) * count, k * head : (k + 1) * head] for k in range(groups)], axis=0)
        for r in range(rows)
    ]
    scores = jnp.concatenate([across(queries[r], keys_ref[r]) for r in range(rows)], axis=0)

    shape = (8 * zs, size)
    note = lax.rem(iota(shape, 0), zs) * 8 + toks
    pairs = jnp.dot(
        jnp.where(iota(shape, 1) == note, 1.0, 0.0).astype(bf16), block[:, :half], preferred_element_type=f32
    )
    shape = (8 * zs, half)
    start = lax.div(iota(shape, 0), zs) * pair_cols
    at = iota(shape, 1)
    pairs = jnp.where((at >= start) & (at < start + pair_cols), pairs, 0.0).astype(bf16)
    shape = (half, 2 * head)
    spread = jnp.where(lax.rem(iota(shape, 0), pair_cols) == lax.rem(iota(shape, 1), pair_cols), 1.0, 0.0)
    pairs = jnp.dot(pairs, spread.astype(bf16), preferred_element_type=f32)
    shape = (8 * zs, 2 * head)
    start = lax.rem(iota(shape, 0), zs) * pair_cols
    at = iota(shape, 1)
    pairs = jnp.where((at >= start) & (at < start + pair_cols), pairs, 0.0).astype(bf16)
    shape = (128, 8 * zs)
    start = iota(shape, 0) * zs
    at = iota(shape, 1)
    fresh = jnp.where((at >= start) & (at < start + zs) & (at < toks * zs), 1.0, 0.0).astype(bf16)
    fresh = jnp.dot(fresh, pairs, preferred_element_type=f32).astype(bf16)

    own = across(jnp.concatenate(queries, axis=0), fresh[:, :head])
    scores = jnp.concatenate([scores, own], axis=1) * head**-0.5
    shape = scores.shape
    at = iota(shape, 1)
    row = lax.div(iota(shape, 0), groups * count)
    token = row * new + lax.rem(iota(shape, 0), new)
    length = jnp.zeros(shape, jnp.int32)
    for r in range(rows):
        length = jnp.where(row == r, lengths_ref[r], length)
    cached = (at < part) & (at + narrow * part < length)
    usable = cached | ((at >= part + row * new) & (at <= part + token) & (narrow == 0))
    scores = jnp.where(usable, scores, masked_score)
    top = scores.max(1, keepdims=True)
    weights = jnp.where(usable, jnp.exp(scores - top), 0.0)
    total = weights.sum(1, keepdims=True)
    weights = weights.astype(bf16)
    size_r = groups * count
    weighted = jnp.concatenate(
        [
            jnp.dot(weights[r * size_r : (r + 1) * size_r, :part], values_ref[r], preferred_element_type=f32)
            for r in range(rows)
        ],
        axis=0,
    )
    weighted = weighted + jnp.dot(weights[:, part:], fresh[:, head:], preferred_element_type=f32)
    weighted = by_group(weighted.astype(bf16))

    shape = (rows * size_r, 128)
    row = lax.div(iota(shape, 0), groups * count)
    at = iota(shape, 1) - row * new - lax.rem(iota(shape, 0), new)
    marks = jnp.zeros(shape, f32)
    for k, value in enumerate(parts_of(top, 3) + parts_of(total, 3)):
        marks = jnp.where(at == k * 8, value, marks)
    marks = by_group(marks.astype(bf16))
    shape = (size, rows * count)
    there, note = place(shape, 1, 0), place(shape, 1, None)
    for k in range(groups):
        piece = jnp.dot(there, weighted[k], preferred_element_type=f32)
        mark = jnp.dot(note, marks[k], preferred_element_type=f32)
        sent_ref[:, k * head : k * head + 128] = (piece[:, :128] + mark).astype(bf16)
        sent_ref[:, k * head + 128 : (k + 1) * head] = piece[:, 128:].astype(bf16)


def last_kernel(toks, per_z, parts_ref, weights_ref, down_ref, mixed_ref):
    ns, rows, cols = parts_ref.shape
    mine = mixed_ref.shape[0]
    zs = rows - mine
    head = cols // per_z
    shape = (ns * mine, ns * zs)
    start = iota(shape, 1) * toks
    at = iota(shape, 0)
    expand = jnp.where((at >= start) & (at < start + toks), 1.0, 0.0).astype(bf16)
    shape = (ns * mine, 128)
    at = iota(shape, 1)
    own = (lax.rem(at, 8) == lax.rem(iota(shape, 0), toks)) & (at < 48)
    at = iota((128, 128), 0)
    pick_top = jnp.where(at < 24, 1.0, 0.0).astype(bf16)
    pick_total = jnp.where((at >= 24) & (at < 48), 1.0, 0.0).astype(bf16)
    mixed = down_ref[0].astype(f32)
    for k in range(1, down_ref.shape[0]):
        mixed = mixed + down_ref[k].astype(f32)
    for k in range(per_z):
        marks = jnp.concatenate([parts_ref[n, mine:, k * head : k * head + 128] for n in range(ns)], axis=0)
        marks = jnp.dot(expand, marks, preferred_element_type=f32)
        marks = jnp.where(own, marks, 0.0).astype(bf16)
        tops = jnp.dot(marks, pick_top, preferred_element_type=f32)
        totals = jnp.dot(marks, pick_total, preferred_element_type=f32)
        tops = [tops[n * mine : (n + 1) * mine] for n in range(ns)]
        top = tops[0]
        for n in range(1, ns):
            top = jnp.maximum(top, tops[n])
        total = jnp.zeros((mine, 128), f32)
        weighted = jnp.zeros((mine, head), f32)
        for n in range(ns):
            scale = jnp.exp(tops[n] - top)
            total = total + totals[n * mine : (n + 1) * mine] * scale
            scale = jnp.concatenate([scale] * (head // 128), axis=1)
            weighted = weighted + parts_ref[n, :mine, k * head : (k + 1) * head].astype(f32) * scale
        total = jnp.concatenate([total] * (head // 128), axis=1)
        attended = (weighted / total).astype(bf16)
        mixed = mixed + jnp.dot(
            attended, weights_ref[k * head : (k + 1) * head], preferred_element_type=f32
        )
    mixed_ref[...] = mixed.astype(bf16)


def local(
    activations,
    norm_gain,
    w_query,
    w_keyval,
    w_out,
    w_gate,
    w_up,
    w_down,
    key_cache,
    value_cache,
    lengths,
):
    zs, ys, ns = lax.axis_size("z"), lax.axis_size("y"), lax.axis_size(NARROW)
    ws = zs * ys
    rows, new, width = activations.shape
    toks = rows * new
    mine = zs * toks
    head_dim = key_cache.shape[2]
    kv_cols = w_keyval.shape[1]
    lanes = w_query.shape[1]
    heads = ws * lanes // head_dim
    cols = ys * lanes
    pair_cols = ys * kv_cols
    per_z = cols // head_dim
    ffn = w_gate.shape[1]

    values = activations.reshape(toks, width).astype(f32)
    gain = norm_gain.reshape(1, width)

    chunks = width // lanes
    pair_lanes = w_keyval.T.reshape(kv_cols, chunks, lanes).transpose(1, 0, 2).reshape(chunks * kv_cols, lanes)
    w_first = lax.all_gather(w_query, "y", axis=0, tiled=False)
    w_pair = lax.all_gather(pair_lanes, "y", axis=0, tiled=False)
    w_last = lax.all_gather(w_out, "y", axis=0, tiled=True)

    packed = activations.reshape(toks * width // 128, 128)
    copies = jnp.broadcast_to(packed[None], (zs,) + packed.shape)
    column = lax.all_to_all(copies, "z", 0, 0, tiled=True)
    column = pl.pallas_call(
        spread_kernel,
        out_shape=jax.ShapeDtypeStruct((ys, mine, width), bf16),
        in_specs=[vmem, vmem],
        out_specs=vmem,
        scratch_shapes=[pltpu.VMEM((mine * width // 128, 128), f32)],
        compiler_params=pltpu.CompilerParams(vmem_limit_bytes=8 * 2**20),
        cost_estimate=pl.CostEstimate(flops=0, bytes_accessed=2**20, transcendentals=0),
        name="spread",
    )(column.reshape(mine * width // 128, 128), w_pair)

    products = pl.pallas_call(
        gains_kernel,
        out_shape=jax.ShapeDtypeStruct((8, 2 * ffn), f32),
        in_specs=[vmem] * 3,
        out_specs=vmem,
        compiler_params=pltpu.CompilerParams(vmem_limit_bytes=8 * 2**20),
        cost_estimate=pl.CostEstimate(flops=2**25, bytes_accessed=2 * 2**20, transcendentals=0),
        name="gains",
    )(gain, w_gate, w_up)
    flat = lax.all_to_all(column, "y", 0, 0, tiled=True).reshape(ys * mine, width)
    parts = pl.pallas_call(
        functools.partial(first_kernel, toks),
        out_shape=jax.ShapeDtypeStruct((mine + zs + 8, cols), bf16),
        in_specs=[vmem] * 5,
        out_specs=vmem,
        compiler_params=pltpu.CompilerParams(vmem_limit_bytes=12 * 2**20),
        cost_estimate=pl.CostEstimate(flops=2 * mine * width * cols, bytes_accessed=2 * 2**20, transcendentals=0),
        name="first",
    )(column, gain, products, w_first, w_pair)

    sums = pl.pallas_call(
        hidden_kernel,
        out_shape=jax.ShapeDtypeStruct((ys * mine, 2 * ffn + 128), f32),
        in_specs=[anywhere] + [vmem] * 5,
        out_specs=anywhere,
        scratch_shapes=[
            pltpu.VMEM((ys * mine, width), bf16),
            pltpu.VMEM((ys * mine, 2 * ffn + 128), f32),
            pltpu.SemaphoreType.DMA((2,)),
            pltpu.SemaphoreType.DMA((2,)),
        ],
        compiler_params=pltpu.CompilerParams(vmem_limit_bytes=16 * 2**20),
        cost_estimate=pl.CostEstimate(flops=2**30, bytes_accessed=4 * 2**20, transcendentals=0),
        name="hidden",
    )(flat, gain, products, w_gate, w_up, parts)
    sums = lax.psum_scatter(sums, NARROW, scatter_dimension=0, tiled=True)

    parts = lax.all_gather(parts, NARROW, axis=0, tiled=False)
    notes = parts
    block = pl.pallas_call(
        functools.partial(second_kernel, toks, width),
        out_shape=jax.ShapeDtypeStruct((zs * 8, cols), bf16),
        in_specs=[vmem],
        out_specs=vmem,
        compiler_params=pltpu.CompilerParams(vmem_limit_bytes=12 * 2**20),
        cost_estimate=pl.CostEstimate(flops=2**24, bytes_accessed=2 * 2**20, transcendentals=0),
        name="second",
    )(parts)
    block = lax.all_to_all(block.reshape(zs, 8, cols), "z", 0, 0, tiled=True)

    block = pl.pallas_call(
        functools.partial(attend_kernel, new),
        out_shape=jax.ShapeDtypeStruct((zs * 8, cols), bf16),
        in_specs=[pl.BlockSpec(memory_space=pltpu.SMEM), vmem, vmem, vmem],
        out_specs=vmem,
        compiler_params=pltpu.CompilerParams(vmem_limit_bytes=12 * 2**20),
        cost_estimate=pl.CostEstimate(flops=2**28, bytes_accessed=2**20, transcendentals=2**16),
        name="attend",
    )(lengths, block.reshape(zs * 8, cols), key_cache, value_cache)
    block = block.reshape(zs, 8, cols)
    block = lax.all_to_all(block, "z", 0, 0, tiled=True)
    parts = jnp.concatenate([block[:, :toks].reshape(mine, cols), block[:, toks]], axis=0)
    parts = lax.all_gather(parts, NARROW, axis=0, tiled=False)
    hidden = pl.pallas_call(
        functools.partial(third_kernel, toks),
        out_shape=jax.ShapeDtypeStruct((sums.shape[0], ffn), bf16),
        in_specs=[vmem, vmem],
        out_specs=vmem,
        compiler_params=pltpu.CompilerParams(vmem_limit_bytes=8 * 2**20),
        cost_estimate=pl.CostEstimate(flops=2**24, bytes_accessed=2 * 2**20, transcendentals=0),
        name="third",
    )(sums, notes)
    hidden = lax.all_gather(hidden, NARROW, axis=0, tiled=True)
    down = jnp.dot(hidden, w_down, preferred_element_type=f32).astype(bf16)
    down = lax.all_to_all(down.reshape(ys, mine, width), "y", 0, 0, tiled=True)

    mixed = pl.pallas_call(
        functools.partial(last_kernel, toks, per_z),
        out_shape=jax.ShapeDtypeStruct((mine, width), bf16),
        in_specs=[vmem, vmem, vmem],
        out_specs=vmem,
        compiler_params=pltpu.CompilerParams(vmem_limit_bytes=12 * 2**20),
        cost_estimate=pl.CostEstimate(
            flops=2 * mine * width * cols, bytes_accessed=3 * 2**20, transcendentals=0
        ),
        name="last",
    )(parts, w_last, down)
    mixed = mixed.reshape(zs, toks * width // 128, 128)
    mixed = lax.all_to_all(mixed, "z", 0, 0, tiled=True)
    mixed = mixed.astype(f32).sum(0).reshape(toks, width)
    return (values + mixed).astype(bf16).reshape(activations.shape)


def solution(mesh):
    names = ("z", "y", "x", "core")
    split = Mesh(mesh.devices.reshape(16, 4, 4, 2), names)
    return jax.shard_map(
        local,
        mesh=split,
        in_specs=(
            P(WIDE, None, NARROW),
            P(NARROW),
            P(NARROW, WIDE),
            P(NARROW, WIDE),
            P(WIDE, NARROW),
            P(NARROW, WIDE),
            P(NARROW, WIDE),
            P(WIDE, NARROW),
            P(WIDE, NARROW, None),
            P(WIDE, NARROW, None),
            P(WIDE),
        ),
        out_specs=P(WIDE, None, NARROW),
        check_vma=False,
    )
```

```python
import functools

import jax
import jax.numpy as jnp
import numpy as np
from jax import lax
from jax.experimental import pallas as pl
from jax.experimental.pallas import tpu as pltpu
from jax.sharding import Mesh
from jax.sharding import PartitionSpec as P

D = 8192
eps_norm = 1e-05
masked_score = -1e30
bf16 = jnp.bfloat16
f32 = jnp.float32
vmem = pl.BlockSpec(memory_space=pltpu.VMEM)
anywhere = pl.BlockSpec(memory_space=pl.ANY)
WIDE = ("z", "y")
NARROW = ("x", "core")


def three_parts(value):
    first = lax.reduce_precision(value, 8, 7)
    rest = value - first
    second = lax.reduce_precision(rest, 8, 7)
    return first, second, lax.reduce_precision(rest - second, 8, 7)


def iota(shape, axis):
    return lax.broadcasted_iota(jnp.int32, shape, axis)


def spread_kernel(packed_ref, pairs_ref, copies_ref, rows_ref):
    del pairs_ref
    ys, mine, width = copies_ref.shape
    chunks = width // 128
    rows_ref[...] = packed_ref[...].astype(f32)
    for j in range(chunks):
        chunk = rows_ref[pl.ds(j, mine, stride=chunks), :].astype(bf16)
        for y in range(ys):
            copies_ref[y, :, j * 128 : (j + 1) * 128] = chunk


def parts_of(value, count):
    found = []
    for _ in range(count):
        found.append(value.astype(bf16).astype(f32))
        value = value - found[-1]
    return found


def gain_rows(gain_ref):
    shape = (8, gain_ref.shape[1])
    rows = jnp.zeros(shape, f32)
    for k, part in enumerate(parts_of(gain_ref[...], 3)):
        rows = jnp.where(iota(shape, 0) == k, part, rows)
    return rows.astype(bf16)


def centred(tokens, gain_ref):
    tokens = tokens.astype(f32)
    total = tokens.sum(1, keepdims=True)
    mean = total * (1.0 / tokens.shape[1])
    squares = (tokens * tokens).sum(1, keepdims=True)
    return ((tokens - mean) * gain_ref[...]).astype(bf16), mean, total, squares


def across(left, right):
    return lax.dot_general(left, right, (((1,), (1,)), ((), ())), preferred_element_type=f32)


def gains_kernel(gain_ref, gate_ref, up_ref, products_ref):
    ffn = gate_ref.shape[1]
    gains = gain_rows(gain_ref)
    for k, ref in enumerate((gate_ref, up_ref)):
        product = jnp.dot(gains, ref[...], preferred_element_type=f32).sum(0, keepdims=True)
        products_ref[:, k * ffn : (k + 1) * ffn] = jnp.broadcast_to(product, (8, ffn))


def hidden_kernel(
    source_ref, gain_ref, products_ref, gate_ref, up_ref, parts_ref, out_ref, tokens_ref, sums_ref, arrived, sent
):
    del parts_ref
    ffn = gate_ref.shape[1]
    pieces = arrived.shape[0]
    count = source_ref.shape[0] // pieces
    lane = iota((count, 128), 1)
    rows = [slice(j * count, (j + 1) * count) for j in range(pieces)]
    reads = [pltpu.make_async_copy(source_ref.at[at], tokens_ref.at[at], arrived.at[j]) for j, at in enumerate(rows)]
    writes = [pltpu.make_async_copy(sums_ref.at[at], out_ref.at[at], sent.at[j]) for j, at in enumerate(rows)]
    for read in reads:
        read.start()
    for j, at in enumerate(rows):
        reads[j].wait()
        ready, mean, total, squares = centred(tokens_ref[at], gain_ref)
        for k, ref in enumerate((gate_ref, up_ref)):
            product = jnp.dot(ready, ref[...], preferred_element_type=f32)
            sums_ref[at, k * ffn : (k + 1) * ffn] = product + mean * products_ref[0:1, k * ffn : (k + 1) * ffn]
        sums_ref[at, 2 * ffn :] = jnp.where(lane == 0, total, jnp.where(lane == 1, squares, 0.0))
        writes[j].start()
    for write in writes:
        write.wait()


def first_kernel(toks, column_ref, gain_ref, notes_ref, weights_ref, pairs_ref, parts_ref):
    ys, mine, width = column_ref.shape
    lanes = weights_ref.shape[2]
    cols = ys * lanes
    half = cols // 2
    zs = mine // toks
    chunks = width // lanes
    column, _, total, squares = centred(column_ref[0], gain_ref)
    gains = gain_rows(gain_ref)
    pairs, products = [], []
    for k in range(ys):
        query = jnp.dot(column, weights_ref[k], preferred_element_type=f32)
        parts_ref[:mine, k * lanes : (k + 1) * lanes] = query.astype(bf16)
        products.append(jnp.dot(gains, weights_ref[k], preferred_element_type=f32))
        rows = pairs_ref[k].astype(f32)
        count = rows.shape[0] // chunks
        pairs.append(jnp.concatenate([rows[j * count : (j + 1) * count] for j in range(chunks)], axis=1))
    pairs = jnp.concatenate(pairs, axis=0)
    count = pairs.shape[0]
    pairs = jnp.concatenate([pairs, jnp.zeros((128 - count, width), f32)], axis=0).astype(bf16)
    pair_products = across(gains, pairs).sum(0, keepdims=True)
    pairs = across(column, pairs).astype(bf16)
    at = iota((128, half), 1)
    spread = jnp.where((lax.rem(at, count) == iota((128, half), 0)) & (at < toks * count), 1.0, 0.0)
    pairs = jnp.dot(pairs, spread.astype(bf16), preferred_element_type=f32)
    start = lax.rem(iota((mine, half), 0), toks) * count
    at = iota((mine, half), 1)
    pairs = jnp.where((at >= start) & (at < start + count), pairs, 0.0).astype(bf16)
    start = iota((zs, mine), 0) * toks
    at = iota((zs, mine), 1)
    collect = jnp.where((at >= start) & (at < start + toks), 1.0, 0.0).astype(bf16)
    pairs = jnp.dot(collect, pairs, preferred_element_type=f32)

    row = iota((zs, half), 0)
    beside = jnp.zeros((zs, half), f32)
    for j in range(4):
        high, low = parts_of(notes_ref[0:1, j * half : (j + 1) * half], 2)
        beside = jnp.where(row == j, high, jnp.where(row == 4 + j, low, beside))
    parts_ref[mine : mine + zs] = jnp.concatenate([pairs, beside], axis=1).astype(bf16)

    row = iota((8, cols), 0)
    tail = jnp.zeros((8, cols), f32)
    for k, value in enumerate((total, squares)):
        value = jnp.concatenate([jnp.broadcast_to(value, (mine, 128)), jnp.zeros((128 - mine, 128), f32)], axis=0)
        value = jnp.concatenate([value.T[0:1], jnp.zeros((1, cols - 128), f32)], axis=1)
        for j, part in enumerate(parts_of(value, 3)):
            tail = jnp.where(row == 3 * k + j, part, tail)
    products = jnp.concatenate(products, axis=1).sum(0, keepdims=True)
    for k, part in enumerate(parts_of(products, 2)):
        tail = jnp.where(row == 6 + k, part, tail)
    pair_products = jnp.concatenate([jnp.zeros((1, cols - 128), f32), pair_products], axis=1)
    for k, part in enumerate(parts_of(pair_products, 2)):
        tail = jnp.where((row == k) & (iota((8, cols), 1) >= cols - 128), part, tail)
    parts_ref[mine + zs :] = tail.astype(bf16)


def pick(shape, group, mask):
    frm, to = iota(shape, 0), iota(shape, 1)
    kind = frm & 7
    same = lax.shift_right_logical(frm, 3) == lax.shift_right_logical(to, group)
    return jnp.where(same & (kind < 3) & mask(to), 1.0, 0.0).astype(bf16)


def norm(tails, count, depth):
    every = tails.shape[1] - 128
    shape = (count, every)
    select = jnp.where(iota(shape, 1) == iota(shape, 0), 1.0, 0.0).astype(bf16)
    own = across(select, tails[:, :every]).astype(bf16)
    kind = iota((tails.shape[0], 128), 0) & 7
    total = jnp.dot(own, jnp.where(kind < 3, 1.0, 0.0).astype(bf16), preferred_element_type=f32)
    centre = total * (1.0 / depth)
    total = jnp.dot(
        own, jnp.where((kind >= 3) & (kind < 6), 1.0, 0.0).astype(bf16), preferred_element_type=f32
    )
    spread = total * (1.0 / depth) - centre * centre
    return own, centre, lax.rsqrt(spread + eps_norm)


def shift(own, centre, group, mask, table, width):
    shape = (own.shape[1], table.shape[0])
    means = jnp.dot(own, pick(shape, group, mask), preferred_element_type=f32) * (1.0 / width)
    shape = (own.shape[0], table.shape[0])
    means = jnp.where(mask(iota(shape, 1)), means - centre[:, : shape[1]], 0.0)
    high, low = parts_of(means, 2)
    return jnp.dot(high.astype(bf16), table, preferred_element_type=f32) + jnp.dot(
        low.astype(bf16), table, preferred_element_type=f32
    )


def tails_of(parts_ref, first):
    ns = parts_ref.shape[0]
    return jnp.concatenate([parts_ref[n, first:].astype(f32) for n in range(ns)], axis=0).astype(bf16)


def combine_kernel(toks, width, parts_ref, copies_ref, mark_ref):
    mark_ref[...] = jnp.zeros_like(mark_ref)
    ns, rows, cols = parts_ref.shape
    half = cols // 2
    zs = (rows - 8) // (toks + 1)
    mine = zs * toks
    every = cols - 128
    tails = tails_of(parts_ref, mine + zs)
    total = parts_ref[0, : mine + zs].astype(f32)
    for n in range(1, ns):
        total = total + parts_ref[n, : mine + zs].astype(f32)
    own, centre, _ = norm(tails, mine, ns * width)
    query = total[:mine] + shift(own, centre, 3, lambda to: (to & 7) >= 6, tails, width)
    query = query.astype(bf16)

    pair_cols = cols // zs
    at = iota((128, half), 1)
    spread = jnp.where((lax.rem(at, pair_cols) == iota((128, half), 0)) & (at < toks * pair_cols), 1.0, 0.0)
    shifted = shift(own, centre, 3, lambda to: (to & 7) < 2, tails[:, every:], width)
    pairs = jnp.zeros((mine, half), f32)
    for part in parts_of(shifted, 2):
        pairs = pairs + jnp.dot(part.astype(bf16), spread.astype(bf16), preferred_element_type=f32)
    start = lax.rem(iota((mine, half), 0), toks) * pair_cols
    at = iota((mine, half), 1)
    pairs = jnp.where((at >= start) & (at < start + pair_cols), pairs, 0.0)
    start = iota((zs, mine), 0) * toks
    at = iota((zs, mine), 1)
    collect = jnp.where((at >= start) & (at < start + toks), 1.0, 0.0).astype(bf16)
    rows_of_z = total[mine:, :half]
    for part in parts_of(pairs, 2):
        rows_of_z = rows_of_z + jnp.dot(collect, part.astype(bf16), preferred_element_type=f32)

    row, at = iota((zs, zs), 0), iota((zs, zs), 1)
    join = jnp.where((row < 8) & ((at & 3) == (row & 3)) & (at < 8), 1.0, 0.0).astype(bf16)
    products = jnp.zeros((zs, half), f32)
    for n in range(ns):
        products = products + jnp.dot(join, parts_ref[n, mine : mine + zs, half:], preferred_element_type=f32)
    high, low = parts_of(products, 2)
    row = iota((zs, half), 0)
    beside = jnp.where(row < 4, high, jnp.where(row < 8, low, 0.0))
    rows_of_z = jnp.concatenate([rows_of_z, beside], axis=1).astype(bf16)

    ends = tails.astype(f32)
    ends = sum(ends[8 * n : 8 * n + 8] for n in range(ns))
    row = iota((8, cols), 0)
    at = iota((8, cols), 1)
    tail = jnp.zeros((8, cols), f32)
    for k in (0, 3):
        value = ends[k : k + 1] + ends[k + 1 : k + 2] + ends[k + 2 : k + 3]
        for j, part in enumerate(parts_of(value, 3)):
            tail = jnp.where((row == k + j) & (at < every), part, tail)
    for j, part in enumerate(parts_of(ends[6:7] + ends[7:8], 2)):
        tail = jnp.where(row == 6 + j, part, tail)
    for j, part in enumerate(parts_of(ends[0:1] + ends[1:2], 2)):
        tail = jnp.where((row == j) & (at >= every), part, tail)
    tail = tail.astype(bf16)
    for x in range(copies_ref.shape[0]):
        copies_ref[x, :mine] = query
        copies_ref[x, mine : mine + zs] = rows_of_z
        copies_ref[x, mine + zs :] = tail


def third_kernel(toks, sums_ref, parts_ref, hidden_ref):
    ns, rows, cols = parts_ref.shape
    ffn = hidden_ref.shape[1]
    half = cols // 2
    zs = (rows - 8) // (toks + 1)
    mine = zs * toks
    besides = jnp.concatenate([parts_ref[n, mine : mine + zs, half:] for n in range(ns)], axis=0)
    at = iota((8, ns * zs), 1) & (zs - 1)
    centre = sums_ref[:, 2 * ffn : 2 * ffn + 1] * (1.0 / D)
    spread = sums_ref[:, 2 * ffn + 1 : 2 * ffn + 2] * (1.0 / D) - centre * centre
    scale = lax.rsqrt(spread + eps_norm)
    for j in range(2):
        both = []
        for k in (j, j + 2):
            take = jnp.where((at == k) | (at == k + 4), 1.0, 0.0).astype(bf16)
            product = jnp.dot(take, besides, preferred_element_type=f32)[0:1]
            both.append((sums_ref[:, k * half : (k + 1) * half] - centre * product) * scale)
        gate, up = both
        hidden_ref[:, j * half : (j + 1) * half] = (gate / (1.0 + jnp.exp(-gate)) * up).astype(bf16)


def second_kernel(toks, width, parts_ref, block_ref):
    ns, rows, cols = parts_ref.shape
    half = cols // 2
    zs = block_ref.shape[0] // 8
    mine = zs * toks
    every = cols - 128
    tails = tails_of(parts_ref, mine + zs)
    total = parts_ref[0, : mine + zs].astype(f32)
    for n in range(1, ns):
        total = total + parts_ref[n, : mine + zs].astype(f32)
    own, centre, scale = norm(tails, mine, D)
    query = total[:mine] + shift(own, centre, 3, lambda to: (to & 7) >= 6, tails, width)
    query = (query * jnp.concatenate([scale] * (cols // 128), axis=1)).astype(bf16)
    start = iota((mine, zs), 1) * toks
    at = iota((mine, zs), 0)
    expand = jnp.where((at >= start) & (at < start + toks), 1.0, 0.0).astype(bf16)
    pairs = jnp.zeros((mine, half), f32)
    for part in parts_of(total[mine:, :half], 3):
        pairs = pairs + jnp.dot(expand, part.astype(bf16), preferred_element_type=f32)
    pair_cols = 2 * cols // zs // 2
    at = iota((128, half), 1)
    spread = jnp.where((lax.rem(at, pair_cols) == iota((128, half), 0)) & (at < toks * pair_cols), 1.0, 0.0)
    shifted = shift(own, centre, 3, lambda to: (to & 7) < 2, tails[:, every:], width)
    for part in parts_of(shifted, 3):
        pairs = pairs + jnp.dot(part.astype(bf16), spread.astype(bf16), preferred_element_type=f32)
    pairs = pairs * jnp.concatenate([scale] * (half // 128), axis=1)
    start = lax.rem(iota((mine, half), 0), toks) * pair_cols
    at = iota((mine, half), 1)
    pairs = jnp.where((at >= start) & (at < start + pair_cols), pairs, 0.0).astype(bf16)
    shape = (zs * 8, mine)
    to, at = iota(shape, 0), iota(shape, 1)
    row = to & 7
    start = lax.shift_right_logical(to, 3) * toks
    take = jnp.where((row < toks) & (at == start + row), 1.0, 0.0).astype(bf16)
    block_ref[...] = jnp.dot(take, query, preferred_element_type=f32).astype(bf16)
    take = jnp.where((row == toks) & (at >= start) & (at < start + toks), 1.0, 0.0).astype(bf16)
    pairs = jnp.dot(take, pairs, preferred_element_type=f32)
    block_ref[:, :half] = (block_ref[:, :half].astype(f32) + pairs).astype(bf16)


def attend_kernel(new, lengths_ref, block_ref, keys_ref, values_ref, sent_ref):
    rows, part, head = keys_ref.shape
    size, cols = block_ref.shape
    zs = size // 8
    toks = rows * new
    groups = cols // head
    pair_cols = 2 * head // zs
    half = cols // 2
    count = zs * new
    narrow = lax.axis_index("x") * lax.axis_size("core") + lax.axis_index("core")
    block = block_ref[...]

    def place(shape, axis, target):
        at = iota(shape, axis)
        row = lax.div(at, count)
        at = at - row * count
        z = lax.div(at, new)
        to = z * 8 + (toks if target is None else row * new + at - z * new)
        return jnp.where(iota(shape, 1 - axis) == to, 1.0, 0.0).astype(bf16)

    def by_group(values):
        return [
            jnp.concatenate([values[(r * groups + k) * count : (r * groups + k + 1) * count] for r in range(rows)], axis=0)
            for k in range(groups)
        ]

    chosen = jnp.dot(place((rows * count, size), 0, 0), block, preferred_element_type=f32).astype(bf16)
    queries = [
        jnp.concatenate([chosen[r * count : (r + 1) * count, k * head : (k + 1) * head] for k in range(groups)], axis=0)
        for r in range(rows)
    ]
    scores = jnp.concatenate([across(queries[r], keys_ref[r]) for r in range(rows)], axis=0)

    shape = (8 * zs, size)
    note = lax.rem(iota(shape, 0), zs) * 8 + toks
    pairs = jnp.dot(
        jnp.where(iota(shape, 1) == note, 1.0, 0.0).astype(bf16), block[:, :half], preferred_element_type=f32
    )
    shape = (8 * zs, half)
    start = lax.div(iota(shape, 0), zs) * pair_cols
    at = iota(shape, 1)
    pairs = jnp.where((at >= start) & (at < start + pair_cols), pairs, 0.0).astype(bf16)
    shape = (half, 2 * head)
    spread = jnp.where(lax.rem(iota(shape, 0), pair_cols) == lax.rem(iota(shape, 1), pair_cols), 1.0, 0.0)
    pairs = jnp.dot(pairs, spread.astype(bf16), preferred_element_type=f32)
    shape = (8 * zs, 2 * head)
    start = lax.rem(iota(shape, 0), zs) * pair_cols
    at = iota(shape, 1)
    pairs = jnp.where((at >= start) & (at < start + pair_cols), pairs, 0.0).astype(bf16)
    shape = (128, 8 * zs)
    start = iota(shape, 0) * zs
    at = iota(shape, 1)
    fresh = jnp.where((at >= start) & (at < start + zs) & (at < toks * zs), 1.0, 0.0).astype(bf16)
    fresh = jnp.dot(fresh, pairs, preferred_element_type=f32).astype(bf16)

    own = across(jnp.concatenate(queries, axis=0), fresh[:, :head])
    scores = jnp.concatenate([scores, own], axis=1) * head**-0.5
    shape = scores.shape
    at = iota(shape, 1)
    row = lax.div(iota(shape, 0), groups * count)
    token = row * new + lax.rem(iota(shape, 0), new)
    length = jnp.zeros(shape, jnp.int32)
    for r in range(rows):
        length = jnp.where(row == r, lengths_ref[r], length)
    cached = (at < part) & (at + narrow * part < length)
    usable = cached | ((at >= part + row * new) & (at <= part + token) & (narrow == 0))
    scores = jnp.where(usable, scores, masked_score)
    top = scores.max(1, keepdims=True)
    weights = jnp.where(usable, jnp.exp(scores - top), 0.0)
    total = weights.sum(1, keepdims=True)
    weights = weights.astype(bf16)
    size_r = groups * count
    weighted = jnp.concatenate(
        [
            jnp.dot(weights[r * size_r : (r + 1) * size_r, :part], values_ref[r], preferred_element_type=f32)
            for r in range(rows)
        ],
        axis=0,
    )
    weighted = weighted + jnp.dot(weights[:, part:], fresh[:, head:], preferred_element_type=f32)
    weighted = by_group(weighted.astype(bf16))

    shape = (rows * size_r, 128)
    row = lax.div(iota(shape, 0), groups * count)
    at = iota(shape, 1) - row * new - lax.rem(iota(shape, 0), new)
    marks = jnp.zeros(shape, f32)
    for k, value in enumerate(parts_of(top, 3) + parts_of(total, 3)):
        marks = jnp.where(at == k * 8, value, marks)
    marks = by_group(marks.astype(bf16))
    shape = (size, rows * count)
    there, note = place(shape, 1, 0), place(shape, 1, None)
    for k in range(groups):
        piece = jnp.dot(there, weighted[k], preferred_element_type=f32)
        mark = jnp.dot(note, marks[k], preferred_element_type=f32)
        sent_ref[:, k * head : k * head + 128] = (piece[:, :128] + mark).astype(bf16)
        sent_ref[:, k * head + 128 : (k + 1) * head] = piece[:, 128:].astype(bf16)


def last_kernel(toks, per_z, parts_ref, weights_ref, down_ref, mixed_ref):
    ns, rows, cols = parts_ref.shape
    mine = mixed_ref.shape[0]
    zs = rows - mine
    head = cols // per_z
    shape = (ns * mine, ns * zs)
    start = iota(shape, 1) * toks
    at = iota(shape, 0)
    expand = jnp.where((at >= start) & (at < start + toks), 1.0, 0.0).astype(bf16)
    shape = (ns * mine, 128)
    at = iota(shape, 1)
    own = (lax.rem(at, 8) == lax.rem(iota(shape, 0), toks)) & (at < 48)
    at = iota((128, 128), 0)
    pick_top = jnp.where(at < 24, 1.0, 0.0).astype(bf16)
    pick_total = jnp.where((at >= 24) & (at < 48), 1.0, 0.0).astype(bf16)
    mixed = down_ref[0].astype(f32)
    for k in range(1, down_ref.shape[0]):
        mixed = mixed + down_ref[k].astype(f32)
    for k in range(per_z):
        marks = jnp.concatenate([parts_ref[n, mine:, k * head : k * head + 128] for n in range(ns)], axis=0)
        marks = jnp.dot(expand, marks, preferred_element_type=f32)
        marks = jnp.where(own, marks, 0.0).astype(bf16)
        tops = jnp.dot(marks, pick_top, preferred_element_type=f32)
        totals = jnp.dot(marks, pick_total, preferred_element_type=f32)
        tops = [tops[n * mine : (n + 1) * mine] for n in range(ns)]
        top = tops[0]
        for n in range(1, ns):
            top = jnp.maximum(top, tops[n])
        total = jnp.zeros((mine, 128), f32)
        weighted = jnp.zeros((mine, head), f32)
        for n in range(ns):
            scale = jnp.exp(tops[n] - top)
            total = total + totals[n * mine : (n + 1) * mine] * scale
            scale = jnp.concatenate([scale] * (head // 128), axis=1)
            weighted = weighted + parts_ref[n, :mine, k * head : (k + 1) * head].astype(f32) * scale
        total = jnp.concatenate([total] * (head // 128), axis=1)
        attended = (weighted / total).astype(bf16)
        mixed = mixed + jnp.dot(
            attended, weights_ref[k * head : (k + 1) * head], preferred_element_type=f32
        )
    mixed_ref[...] = mixed.astype(bf16)


def local(
    activations,
    norm_gain,
    w_query,
    w_keyval,
    w_out,
    w_gate,
    w_up,
    w_down,
    key_cache,
    value_cache,
    lengths,
):
    zs, ys, ns = lax.axis_size("z"), lax.axis_size("y"), lax.axis_size(NARROW)
    ws = zs * ys
    rows, new, width = activations.shape
    toks = rows * new
    mine = zs * toks
    head_dim = key_cache.shape[2]
    kv_cols = w_keyval.shape[1]
    lanes = w_query.shape[1]
    heads = ws * lanes // head_dim
    cols = ys * lanes
    pair_cols = ys * kv_cols
    per_z = cols // head_dim
    ffn = w_gate.shape[1]

    values = activations.reshape(toks, width).astype(f32)
    gain = norm_gain.reshape(1, width)

    chunks = width // lanes
    pair_lanes = w_keyval.T.reshape(kv_cols, chunks, lanes).transpose(1, 0, 2).reshape(chunks * kv_cols, lanes)
    w_first = lax.all_gather(w_query, "y", axis=0, tiled=False)
    w_pair = lax.all_gather(pair_lanes, "y", axis=0, tiled=False)
    w_last = lax.all_gather(w_out, "y", axis=0, tiled=True)

    packed = activations.reshape(toks * width // 128, 128)
    copies = jnp.broadcast_to(packed[None], (zs,) + packed.shape)
    column = lax.all_to_all(copies, "z", 0, 0, tiled=True)
    column = pl.pallas_call(
        spread_kernel,
        out_shape=jax.ShapeDtypeStruct((ys, mine, width), bf16),
        in_specs=[vmem, vmem],
        out_specs=vmem,
        scratch_shapes=[pltpu.VMEM((mine * width // 128, 128), f32)],
        compiler_params=pltpu.CompilerParams(vmem_limit_bytes=8 * 2**20),
        cost_estimate=pl.CostEstimate(flops=0, bytes_accessed=2**20, transcendentals=0),
        name="spread",
    )(column.reshape(mine * width // 128, 128), w_pair)

    products = pl.pallas_call(
        gains_kernel,
        out_shape=jax.ShapeDtypeStruct((8, 2 * ffn), f32),
        in_specs=[vmem] * 3,
        out_specs=vmem,
        compiler_params=pltpu.CompilerParams(vmem_limit_bytes=5 * 2**20),
        cost_estimate=pl.CostEstimate(flops=2**25, bytes_accessed=2 * 2**20, transcendentals=0),
        name="gains",
    )(gain, w_gate, w_up)
    flat = lax.all_to_all(column, "y", 0, 0, tiled=True).reshape(ys * mine, width)
    parts = pl.pallas_call(
        functools.partial(first_kernel, toks),
        out_shape=jax.ShapeDtypeStruct((mine + zs + 8, cols), bf16),
        in_specs=[vmem] * 5,
        out_specs=vmem,
        compiler_params=pltpu.CompilerParams(vmem_limit_bytes=6 * 2**20),
        cost_estimate=pl.CostEstimate(flops=2 * mine * width * cols, bytes_accessed=2 * 2**20, transcendentals=0),
        name="first",
    )(column, gain, products, w_first, w_pair)

    parts = lax.all_gather(parts, "core", axis=0, tiled=False)
    copies, mark = pl.pallas_call(
        functools.partial(combine_kernel, toks, width),
        out_shape=(
            jax.ShapeDtypeStruct((ns // 2,) + parts.shape[1:], bf16),
            jax.ShapeDtypeStruct((8, 128), f32),
        ),
        in_specs=[vmem],
        out_specs=(vmem, vmem),
        compiler_params=pltpu.CompilerParams(vmem_limit_bytes=5 * 2**20),
        cost_estimate=pl.CostEstimate(flops=2**24, bytes_accessed=2**20, transcendentals=0),
        name="combine",
    )(parts)

    sums = pl.pallas_call(
        hidden_kernel,
        out_shape=jax.ShapeDtypeStruct((ys * mine, 2 * ffn + 128), f32),
        in_specs=[anywhere] + [vmem] * 5,
        out_specs=anywhere,
        scratch_shapes=[
            pltpu.VMEM((ys * mine, width), bf16),
            pltpu.VMEM((ys * mine, 2 * ffn + 128), f32),
            pltpu.SemaphoreType.DMA((2,)),
            pltpu.SemaphoreType.DMA((2,)),
        ],
        compiler_params=pltpu.CompilerParams(vmem_limit_bytes=10 * 2**20),
        cost_estimate=pl.CostEstimate(flops=2**30, bytes_accessed=4 * 2**20, transcendentals=0),
        name="hidden",
    )(flat, gain, products, w_gate, w_up, mark)
    sums = lax.psum_scatter(sums, NARROW, scatter_dimension=0, tiled=True)

    parts = lax.all_to_all(copies, "x", 0, 0, tiled=True)
    notes = parts
    block = pl.pallas_call(
        functools.partial(second_kernel, toks, 2 * width),
        out_shape=jax.ShapeDtypeStruct((zs * 8, cols), bf16),
        in_specs=[vmem],
        out_specs=vmem,
        compiler_params=pltpu.CompilerParams(vmem_limit_bytes=6 * 2**20),
        cost_estimate=pl.CostEstimate(flops=2**24, bytes_accessed=2 * 2**20, transcendentals=0),
        name="second",
    )(parts)
    block = lax.all_to_all(block.reshape(zs, 8, cols), "z", 0, 0, tiled=True)

    block = pl.pallas_call(
        functools.partial(attend_kernel, new),
        out_shape=jax.ShapeDtypeStruct((zs * 8, cols), bf16),
        in_specs=[pl.BlockSpec(memory_space=pltpu.SMEM), vmem, vmem, vmem],
        out_specs=vmem,
        compiler_params=pltpu.CompilerParams(vmem_limit_bytes=12 * 2**20),
        cost_estimate=pl.CostEstimate(flops=2**28, bytes_accessed=2**20, transcendentals=2**16),
        name="attend",
    )(lengths, block.reshape(zs * 8, cols), key_cache, value_cache)
    block = block.reshape(zs, 8, cols)
    block = lax.all_to_all(block, "z", 0, 0, tiled=True)
    parts = jnp.concatenate([block[:, :toks].reshape(mine, cols), block[:, toks]], axis=0)
    parts = lax.all_gather(parts, NARROW, axis=0, tiled=False)
    hidden = pl.pallas_call(
        functools.partial(third_kernel, toks),
        out_shape=jax.ShapeDtypeStruct((sums.shape[0], ffn), bf16),
        in_specs=[vmem, vmem],
        out_specs=vmem,
        compiler_params=pltpu.CompilerParams(vmem_limit_bytes=5 * 2**20),
        cost_estimate=pl.CostEstimate(flops=2**24, bytes_accessed=2 * 2**20, transcendentals=0),
        name="third",
    )(sums, notes)
    hidden = lax.all_gather(hidden, NARROW, axis=0, tiled=True)
    down = jnp.dot(hidden, w_down, preferred_element_type=f32).astype(bf16)
    down = lax.all_to_all(down.reshape(ys, mine, width), "y", 0, 0, tiled=True)

    mixed = pl.pallas_call(
        functools.partial(last_kernel, toks, per_z),
        out_shape=jax.ShapeDtypeStruct((mine, width), bf16),
        in_specs=[vmem, vmem, vmem],
        out_specs=vmem,
        compiler_params=pltpu.CompilerParams(vmem_limit_bytes=12 * 2**20),
        cost_estimate=pl.CostEstimate(
            flops=2 * mine * width * cols, bytes_accessed=3 * 2**20, transcendentals=0
        ),
        name="last",
    )(parts, w_last, down)
    mixed = mixed.reshape(zs, toks * width // 128, 128)
    mixed = lax.all_to_all(mixed, "z", 0, 0, tiled=True)
    mixed = mixed.astype(f32).sum(0).reshape(toks, width)
    return (values + mixed).astype(bf16).reshape(activations.shape)


def solution(mesh):
    names = ("z", "y", "x", "core")
    split = Mesh(mesh.devices.reshape(16, 4, 4, 2), names)
    return jax.shard_map(
        local,
        mesh=split,
        in_specs=(
            P(WIDE, None, NARROW),
            P(NARROW),
            P(NARROW, WIDE),
            P(NARROW, WIDE),
            P(WIDE, NARROW),
            P(NARROW, WIDE),
            P(NARROW, WIDE),
            P(WIDE, NARROW),
            P(WIDE, NARROW, None),
            P(WIDE, NARROW, None),
            P(WIDE),
        ),
        out_specs=P(WIDE, None, NARROW),
        check_vma=False,
    )
```

```python
import functools

import jax
import jax.numpy as jnp
import numpy as np
from jax import lax
from jax.experimental import pallas as pl
from jax.experimental.pallas import tpu as pltpu
from jax.sharding import Mesh
from jax.sharding import PartitionSpec as P

D = 8192
eps_norm = 1e-05
masked_score = -1e30
bf16 = jnp.bfloat16
f32 = jnp.float32
vmem = pl.BlockSpec(memory_space=pltpu.VMEM)
anywhere = pl.BlockSpec(memory_space=pl.ANY)
WIDE = ("z", "y")
NARROW = ("x", "core")


def three_parts(value):
    first = lax.reduce_precision(value, 8, 7)
    rest = value - first
    second = lax.reduce_precision(rest, 8, 7)
    return first, second, lax.reduce_precision(rest - second, 8, 7)


def iota(shape, axis):
    return lax.broadcasted_iota(jnp.int32, shape, axis)


def spread_kernel(packed_ref, pairs_ref, copies_ref, rows_ref):
    del pairs_ref
    ys, mine, width = copies_ref.shape
    chunks = width // 128
    rows_ref[...] = packed_ref[...].astype(f32)
    for j in range(chunks):
        chunk = rows_ref[pl.ds(j, mine, stride=chunks), :].astype(bf16)
        for y in range(ys):
            copies_ref[y, :, j * 128 : (j + 1) * 128] = chunk


def parts_of(value, count):
    found = []
    for _ in range(count):
        found.append(value.astype(bf16).astype(f32))
        value = value - found[-1]
    return found


def gain_rows(gain_ref):
    shape = (8, gain_ref.shape[1])
    rows = jnp.zeros(shape, f32)
    for k, part in enumerate(parts_of(gain_ref[...], 3)):
        rows = jnp.where(iota(shape, 0) == k, part, rows)
    return rows.astype(bf16)


def centred(tokens, gain_ref):
    tokens = tokens.astype(f32)
    total = tokens.sum(1, keepdims=True)
    mean = total * (1.0 / tokens.shape[1])
    squares = (tokens * tokens).sum(1, keepdims=True)
    return ((tokens - mean) * gain_ref[...]).astype(bf16), mean, total, squares


def across(left, right):
    return lax.dot_general(left, right, (((1,), (1,)), ((), ())), preferred_element_type=f32)


def gains_kernel(gain_ref, gate_ref, up_ref, products_ref):
    ffn = gate_ref.shape[1]
    gains = gain_rows(gain_ref)
    for k, ref in enumerate((gate_ref, up_ref)):
        product = jnp.dot(gains, ref[...], preferred_element_type=f32).sum(0, keepdims=True)
        products_ref[:, k * ffn : (k + 1) * ffn] = jnp.broadcast_to(product, (8, ffn))


def hidden_kernel(
    source_ref, gain_ref, products_ref, gate_ref, up_ref, parts_ref, out_ref, tokens_ref, sums_ref, arrived, sent
):
    del parts_ref
    ffn = gate_ref.shape[1]
    pieces = arrived.shape[0]
    count = source_ref.shape[0] // pieces
    lane = iota((count, 128), 1)
    rows = [slice(j * count, (j + 1) * count) for j in range(pieces)]
    reads = [pltpu.make_async_copy(source_ref.at[at], tokens_ref.at[at], arrived.at[j]) for j, at in enumerate(rows)]
    writes = [pltpu.make_async_copy(sums_ref.at[at], out_ref.at[at], sent.at[j]) for j, at in enumerate(rows)]
    for read in reads:
        read.start()
    for j, at in enumerate(rows):
        reads[j].wait()
        ready, mean, total, squares = centred(tokens_ref[at], gain_ref)
        for k, ref in enumerate((gate_ref, up_ref)):
            product = jnp.dot(ready, ref[...], preferred_element_type=f32)
            sums_ref[at, k * ffn : (k + 1) * ffn] = product + mean * products_ref[0:1, k * ffn : (k + 1) * ffn]
        sums_ref[at, 2 * ffn :] = jnp.where(lane == 0, total, jnp.where(lane == 1, squares, 0.0))
        writes[j].start()
    for write in writes:
        write.wait()


def first_kernel(toks, column_ref, gain_ref, notes_ref, weights_ref, pairs_ref, parts_ref):
    ys, mine, width = column_ref.shape
    lanes = weights_ref.shape[2]
    cols = ys * lanes
    half = cols // 2
    zs = mine // toks
    chunks = width // lanes
    column, _, total, squares = centred(column_ref[0], gain_ref)
    gains = gain_rows(gain_ref)
    pairs, products = [], []
    for k in range(ys):
        query = jnp.dot(column, weights_ref[k], preferred_element_type=f32)
        parts_ref[:mine, k * lanes : (k + 1) * lanes] = query.astype(bf16)
        products.append(jnp.dot(gains, weights_ref[k], preferred_element_type=f32))
        rows = pairs_ref[k].astype(f32)
        count = rows.shape[0] // chunks
        pairs.append(jnp.concatenate([rows[j * count : (j + 1) * count] for j in range(chunks)], axis=1))
    pairs = jnp.concatenate(pairs, axis=0)
    count = pairs.shape[0]
    pairs = jnp.concatenate([pairs, jnp.zeros((128 - count, width), f32)], axis=0).astype(bf16)
    pair_products = across(gains, pairs).sum(0, keepdims=True)
    pairs = across(column, pairs).astype(bf16)
    at = iota((128, half), 1)
    spread = jnp.where((lax.rem(at, count) == iota((128, half), 0)) & (at < toks * count), 1.0, 0.0)
    pairs = jnp.dot(pairs, spread.astype(bf16), preferred_element_type=f32)
    start = lax.rem(iota((mine, half), 0), toks) * count
    at = iota((mine, half), 1)
    pairs = jnp.where((at >= start) & (at < start + count), pairs, 0.0).astype(bf16)
    start = iota((zs, mine), 0) * toks
    at = iota((zs, mine), 1)
    collect = jnp.where((at >= start) & (at < start + toks), 1.0, 0.0).astype(bf16)
    pairs = jnp.dot(collect, pairs, preferred_element_type=f32)

    row = iota((zs, half), 0)
    beside = jnp.zeros((zs, half), f32)
    for j in range(4):
        high, low = parts_of(notes_ref[0:1, j * half : (j + 1) * half], 2)
        beside = jnp.where(row == j, high, jnp.where(row == 4 + j, low, beside))
    parts_ref[mine : mine + zs] = jnp.concatenate([pairs, beside], axis=1).astype(bf16)

    row = iota((8, cols), 0)
    tail = jnp.zeros((8, cols), f32)
    for k, value in enumerate((total, squares)):
        value = jnp.concatenate([jnp.broadcast_to(value, (mine, 128)), jnp.zeros((128 - mine, 128), f32)], axis=0)
        value = jnp.concatenate([value.T[0:1], jnp.zeros((1, cols - 128), f32)], axis=1)
        for j, part in enumerate(parts_of(value, 3)):
            tail = jnp.where(row == 3 * k + j, part, tail)
    products = jnp.concatenate(products, axis=1).sum(0, keepdims=True)
    for k, part in enumerate(parts_of(products, 2)):
        tail = jnp.where(row == 6 + k, part, tail)
    pair_products = jnp.concatenate([jnp.zeros((1, cols - 128), f32), pair_products], axis=1)
    for k, part in enumerate(parts_of(pair_products, 2)):
        tail = jnp.where((row == k) & (iota((8, cols), 1) >= cols - 128), part, tail)
    parts_ref[mine + zs :] = tail.astype(bf16)


def pick(shape, group, mask):
    frm, to = iota(shape, 0), iota(shape, 1)
    kind = frm & 7
    same = lax.shift_right_logical(frm, 3) == lax.shift_right_logical(to, group)
    return jnp.where(same & (kind < 3) & mask(to), 1.0, 0.0).astype(bf16)


def norm(tails, count, depth):
    every = tails.shape[1] - 128
    shape = (count, every)
    select = jnp.where(iota(shape, 1) == iota(shape, 0), 1.0, 0.0).astype(bf16)
    own = across(select, tails[:, :every]).astype(bf16)
    kind = iota((tails.shape[0], 128), 0) & 7
    total = jnp.dot(own, jnp.where(kind < 3, 1.0, 0.0).astype(bf16), preferred_element_type=f32)
    centre = total * (1.0 / depth)
    total = jnp.dot(
        own, jnp.where((kind >= 3) & (kind < 6), 1.0, 0.0).astype(bf16), preferred_element_type=f32
    )
    spread = total * (1.0 / depth) - centre * centre
    return own, centre, lax.rsqrt(spread + eps_norm)


def shift(own, centre, group, mask, table, width):
    shape = (own.shape[1], table.shape[0])
    means = jnp.dot(own, pick(shape, group, mask), preferred_element_type=f32) * (1.0 / width)
    shape = (own.shape[0], table.shape[0])
    means = jnp.where(mask(iota(shape, 1)), means - centre[:, : shape[1]], 0.0)
    high, low = parts_of(means, 2)
    return jnp.dot(high.astype(bf16), table, preferred_element_type=f32) + jnp.dot(
        low.astype(bf16), table, preferred_element_type=f32
    )


def tails_of(parts_ref, first):
    ns = parts_ref.shape[0]
    return jnp.concatenate([parts_ref[n, first:].astype(f32) for n in range(ns)], axis=0).astype(bf16)


def combine_kernel(toks, width, parts_ref, copies_ref, mark_ref):
    mark_ref[...] = jnp.zeros_like(mark_ref)
    ns, rows, cols = parts_ref.shape
    half = cols // 2
    zs = (rows - 8) // (toks + 1)
    mine = zs * toks
    every = cols - 128
    tails = tails_of(parts_ref, mine + zs)
    total = parts_ref[0, : mine + zs].astype(f32)
    for n in range(1, ns):
        total = total + parts_ref[n, : mine + zs].astype(f32)
    own, centre, _ = norm(tails, mine, ns * width)
    query = total[:mine] + shift(own, centre, 3, lambda to: (to & 7) >= 6, tails, width)
    query = query.astype(bf16)

    pair_cols = cols // zs
    at = iota((128, half), 1)
    spread = jnp.where((lax.rem(at, pair_cols) == iota((128, half), 0)) & (at < toks * pair_cols), 1.0, 0.0)
    shifted = shift(own, centre, 3, lambda to: (to & 7) < 2, tails[:, every:], width)
    pairs = jnp.zeros((mine, half), f32)
    for part in parts_of(shifted, 2):
        pairs = pairs + jnp.dot(part.astype(bf16), spread.astype(bf16), preferred_element_type=f32)
    start = lax.rem(iota((mine, half), 0), toks) * pair_cols
    at = iota((mine, half), 1)
    pairs = jnp.where((at >= start) & (at < start + pair_cols), pairs, 0.0)
    start = iota((zs, mine), 0) * toks
    at = iota((zs, mine), 1)
    collect = jnp.where((at >= start) & (at < start + toks), 1.0, 0.0).astype(bf16)
    rows_of_z = total[mine:, :half]
    for part in parts_of(pairs, 2):
        rows_of_z = rows_of_z + jnp.dot(collect, part.astype(bf16), preferred_element_type=f32)

    row, at = iota((zs, zs), 0), iota((zs, zs), 1)
    join = jnp.where((row < 8) & ((at & 3) == (row & 3)) & (at < 8), 1.0, 0.0).astype(bf16)
    products = jnp.zeros((zs, half), f32)
    for n in range(ns):
        products = products + jnp.dot(join, parts_ref[n, mine : mine + zs, half:], preferred_element_type=f32)
    high, low = parts_of(products, 2)
    row = iota((zs, half), 0)
    beside = jnp.where(row < 4, high, jnp.where(row < 8, low, 0.0))
    rows_of_z = jnp.concatenate([rows_of_z, beside], axis=1).astype(bf16)

    ends = tails.astype(f32)
    ends = sum(ends[8 * n : 8 * n + 8] for n in range(ns))
    row = iota((8, cols), 0)
    at = iota((8, cols), 1)
    tail = jnp.zeros((8, cols), f32)
    for k in (0, 3):
        value = ends[k : k + 1] + ends[k + 1 : k + 2] + ends[k + 2 : k + 3]
        for j, part in enumerate(parts_of(value, 3)):
            tail = jnp.where((row == k + j) & (at < every), part, tail)
    for j, part in enumerate(parts_of(ends[6:7] + ends[7:8], 2)):
        tail = jnp.where(row == 6 + j, part, tail)
    for j, part in enumerate(parts_of(ends[0:1] + ends[1:2], 2)):
        tail = jnp.where((row == j) & (at >= every), part, tail)
    tail = tail.astype(bf16)
    for x in range(copies_ref.shape[0]):
        copies_ref[x, :mine] = query
        copies_ref[x, mine : mine + zs] = rows_of_z
        copies_ref[x, mine + zs :] = tail


def third_kernel(toks, sums_ref, parts_ref, hidden_ref):
    ns, rows, cols = parts_ref.shape
    ffn = hidden_ref.shape[1]
    half = cols // 2
    zs = (rows - 8) // (toks + 1)
    mine = zs * toks
    besides = jnp.concatenate([parts_ref[n, mine : mine + zs, half:] for n in range(ns)], axis=0)
    at = iota((8, ns * zs), 1) & (zs - 1)
    centre = sums_ref[:, 2 * ffn : 2 * ffn + 1] * (1.0 / D)
    spread = sums_ref[:, 2 * ffn + 1 : 2 * ffn + 2] * (1.0 / D) - centre * centre
    scale = lax.rsqrt(spread + eps_norm)
    for j in range(2):
        both = []
        for k in (j, j + 2):
            take = jnp.where((at == k) | (at == k + 4), 1.0, 0.0).astype(bf16)
            product = jnp.dot(take, besides, preferred_element_type=f32)[0:1]
            both.append((sums_ref[:, k * half : (k + 1) * half] - centre * product) * scale)
        gate, up = both
        hidden_ref[:, j * half : (j + 1) * half] = (gate / (1.0 + jnp.exp(-gate)) * up).astype(bf16)


def second_kernel(toks, width, parts_ref, block_ref):
    ns, rows, cols = parts_ref.shape
    half = cols // 2
    zs = block_ref.shape[0] // 8
    mine = zs * toks
    every = cols - 128
    tails = tails_of(parts_ref, mine + zs)
    total = parts_ref[0, : mine + zs].astype(f32)
    for n in range(1, ns):
        total = total + parts_ref[n, : mine + zs].astype(f32)
    own, centre, scale = norm(tails, mine, D)
    query = total[:mine] + shift(own, centre, 3, lambda to: (to & 7) >= 6, tails, width)
    query = (query * jnp.concatenate([scale] * (cols // 128), axis=1)).astype(bf16)
    start = iota((mine, zs), 1) * toks
    at = iota((mine, zs), 0)
    expand = jnp.where((at >= start) & (at < start + toks), 1.0, 0.0).astype(bf16)
    pairs = jnp.zeros((mine, half), f32)
    for part in parts_of(total[mine:, :half], 3):
        pairs = pairs + jnp.dot(expand, part.astype(bf16), preferred_element_type=f32)
    pair_cols = 2 * cols // zs // 2
    at = iota((128, half), 1)
    spread = jnp.where((lax.rem(at, pair_cols) == iota((128, half), 0)) & (at < toks * pair_cols), 1.0, 0.0)
    shifted = shift(own, centre, 3, lambda to: (to & 7) < 2, tails[:, every:], width)
    for part in parts_of(shifted, 3):
        pairs = pairs + jnp.dot(part.astype(bf16), spread.astype(bf16), preferred_element_type=f32)
    pairs = pairs * jnp.concatenate([scale] * (half // 128), axis=1)
    start = lax.rem(iota((mine, half), 0), toks) * pair_cols
    at = iota((mine, half), 1)
    pairs = jnp.where((at >= start) & (at < start + pair_cols), pairs, 0.0).astype(bf16)
    shape = (zs * 8, mine)
    to, at = iota(shape, 0), iota(shape, 1)
    row = to & 7
    start = lax.shift_right_logical(to, 3) * toks
    take = jnp.where((row < toks) & (at == start + row), 1.0, 0.0).astype(bf16)
    block_ref[...] = jnp.dot(take, query, preferred_element_type=f32).astype(bf16)
    take = jnp.where((row == toks) & (at >= start) & (at < start + toks), 1.0, 0.0).astype(bf16)
    pairs = jnp.dot(take, pairs, preferred_element_type=f32)
    block_ref[:, :half] = (block_ref[:, :half].astype(f32) + pairs).astype(bf16)


def attend_kernel(new, lengths_ref, block_ref, keys_ref, values_ref, sent_ref):
    rows, part, head = keys_ref.shape
    size, cols = block_ref.shape
    zs = size // 8
    toks = rows * new
    groups = cols // head
    pair_cols = 2 * head // zs
    half = cols // 2
    count = zs * new
    narrow = lax.axis_index("x") * lax.axis_size("core") + lax.axis_index("core")
    block = block_ref[...]

    def place(shape, axis, target):
        at = iota(shape, axis)
        row = lax.div(at, count)
        at = at - row * count
        z = lax.div(at, new)
        to = z * 8 + (toks if target is None else row * new + at - z * new)
        return jnp.where(iota(shape, 1 - axis) == to, 1.0, 0.0).astype(bf16)

    def by_group(values):
        return [
            jnp.concatenate([values[(r * groups + k) * count : (r * groups + k + 1) * count] for r in range(rows)], axis=0)
            for k in range(groups)
        ]

    chosen = jnp.dot(place((rows * count, size), 0, 0), block, preferred_element_type=f32).astype(bf16)
    queries = [
        jnp.concatenate([chosen[r * count : (r + 1) * count, k * head : (k + 1) * head] for k in range(groups)], axis=0)
        for r in range(rows)
    ]
    scores = jnp.concatenate([across(queries[r], keys_ref[r]) for r in range(rows)], axis=0)

    shape = (8 * zs, size)
    note = lax.rem(iota(shape, 0), zs) * 8 + toks
    pairs = jnp.dot(
        jnp.where(iota(shape, 1) == note, 1.0, 0.0).astype(bf16), block[:, :half], preferred_element_type=f32
    )
    shape = (8 * zs, half)
    start = lax.div(iota(shape, 0), zs) * pair_cols
    at = iota(shape, 1)
    pairs = jnp.where((at >= start) & (at < start + pair_cols), pairs, 0.0).astype(bf16)
    shape = (half, 2 * head)
    spread = jnp.where(lax.rem(iota(shape, 0), pair_cols) == lax.rem(iota(shape, 1), pair_cols), 1.0, 0.0)
    pairs = jnp.dot(pairs, spread.astype(bf16), preferred_element_type=f32)
    shape = (8 * zs, 2 * head)
    start = lax.rem(iota(shape, 0), zs) * pair_cols
    at = iota(shape, 1)
    pairs = jnp.where((at >= start) & (at < start + pair_cols), pairs, 0.0).astype(bf16)
    shape = (128, 8 * zs)
    start = iota(shape, 0) * zs
    at = iota(shape, 1)
    fresh = jnp.where((at >= start) & (at < start + zs) & (at < toks * zs), 1.0, 0.0).astype(bf16)
    fresh = jnp.dot(fresh, pairs, preferred_element_type=f32).astype(bf16)

    own = across(jnp.concatenate(queries, axis=0), fresh[:, :head])
    scores = jnp.concatenate([scores, own], axis=1) * head**-0.5
    shape = scores.shape
    at = iota(shape, 1)
    row = lax.div(iota(shape, 0), groups * count)
    token = row * new + lax.rem(iota(shape, 0), new)
    length = jnp.zeros(shape, jnp.int32)
    for r in range(rows):
        length = jnp.where(row == r, lengths_ref[r], length)
    cached = (at < part) & (at + narrow * part < length)
    usable = cached | ((at >= part + row * new) & (at <= part + token) & (narrow == 0))
    scores = jnp.where(usable, scores, masked_score)
    top = scores.max(1, keepdims=True)
    weights = jnp.where(usable, jnp.exp(scores - top), 0.0)
    total = weights.sum(1, keepdims=True)
    weights = weights.astype(bf16)
    size_r = groups * count
    weighted = jnp.concatenate(
        [
            jnp.dot(weights[r * size_r : (r + 1) * size_r, :part], values_ref[r], preferred_element_type=f32)
            for r in range(rows)
        ],
        axis=0,
    )
    weighted = weighted + jnp.dot(weights[:, part:], fresh[:, head:], preferred_element_type=f32)
    weighted = by_group(weighted.astype(bf16))

    shape = (rows * size_r, 128)
    row = lax.div(iota(shape, 0), groups * count)
    at = iota(shape, 1) - row * new - lax.rem(iota(shape, 0), new)
    marks = jnp.zeros(shape, f32)
    for k, value in enumerate(parts_of(top, 3) + parts_of(total, 3)):
        marks = jnp.where(at == k * 8, value, marks)
    marks = by_group(marks.astype(bf16))
    shape = (size, rows * count)
    there, note = place(shape, 1, 0), place(shape, 1, None)
    for k in range(groups):
        piece = jnp.dot(there, weighted[k], preferred_element_type=f32)
        mark = jnp.dot(note, marks[k], preferred_element_type=f32)
        sent_ref[:, k * head : k * head + 128] = (piece[:, :128] + mark).astype(bf16)
        sent_ref[:, k * head + 128 : (k + 1) * head] = piece[:, 128:].astype(bf16)


def last_kernel(toks, per_z, parts_ref, weights_ref, down_ref, mixed_ref):
    ns, rows, cols = parts_ref.shape
    mine = mixed_ref.shape[0]
    zs = rows - mine
    head = cols // per_z
    shape = (ns * mine, ns * zs)
    start = iota(shape, 1) * toks
    at = iota(shape, 0)
    expand = jnp.where((at >= start) & (at < start + toks), 1.0, 0.0).astype(bf16)
    shape = (ns * mine, 128)
    at = iota(shape, 1)
    own = (lax.rem(at, 8) == lax.rem(iota(shape, 0), toks)) & (at < 48)
    at = iota((128, 128), 0)
    pick_top = jnp.where(at < 24, 1.0, 0.0).astype(bf16)
    pick_total = jnp.where((at >= 24) & (at < 48), 1.0, 0.0).astype(bf16)
    mixed = down_ref[0].astype(f32)
    for k in range(1, down_ref.shape[0]):
        mixed = mixed + down_ref[k].astype(f32)
    for k in range(per_z):
        marks = jnp.concatenate([parts_ref[n, mine:, k * head : k * head + 128] for n in range(ns)], axis=0)
        marks = jnp.dot(expand, marks, preferred_element_type=f32)
        marks = jnp.where(own, marks, 0.0).astype(bf16)
        tops = jnp.dot(marks, pick_top, preferred_element_type=f32)
        totals = jnp.dot(marks, pick_total, preferred_element_type=f32)
        tops = [tops[n * mine : (n + 1) * mine] for n in range(ns)]
        top = tops[0]
        for n in range(1, ns):
            top = jnp.maximum(top, tops[n])
        total = jnp.zeros((mine, 128), f32)
        weighted = jnp.zeros((mine, head), f32)
        for n in range(ns):
            scale = jnp.exp(tops[n] - top)
            total = total + totals[n * mine : (n + 1) * mine] * scale
            scale = jnp.concatenate([scale] * (head // 128), axis=1)
            weighted = weighted + parts_ref[n, :mine, k * head : (k + 1) * head].astype(f32) * scale
        total = jnp.concatenate([total] * (head // 128), axis=1)
        attended = (weighted / total).astype(bf16)
        mixed = mixed + jnp.dot(
            attended, weights_ref[k * head : (k + 1) * head], preferred_element_type=f32
        )
    mixed_ref[...] = mixed.astype(bf16)


def local(
    activations,
    norm_gain,
    w_query,
    w_keyval,
    w_out,
    w_gate,
    w_up,
    w_down,
    key_cache,
    value_cache,
    lengths,
):
    zs, ys, ns = lax.axis_size("z"), lax.axis_size("y"), lax.axis_size(NARROW)
    ws = zs * ys
    rows, new, width = activations.shape
    toks = rows * new
    mine = zs * toks
    head_dim = key_cache.shape[2]
    kv_cols = w_keyval.shape[1]
    lanes = w_query.shape[1]
    heads = ws * lanes // head_dim
    cols = ys * lanes
    pair_cols = ys * kv_cols
    per_z = cols // head_dim
    ffn = w_gate.shape[1]

    values = activations.reshape(toks, width).astype(f32)
    gain = norm_gain.reshape(1, width)

    chunks = width // lanes
    pair_lanes = w_keyval.T.reshape(kv_cols, chunks, lanes).transpose(1, 0, 2).reshape(chunks * kv_cols, lanes)
    w_first = lax.all_gather(w_query, "y", axis=0, tiled=False)
    w_pair = lax.all_gather(pair_lanes, "y", axis=0, tiled=False)
    w_last = lax.all_gather(w_out, "y", axis=0, tiled=True)

    packed = activations.reshape(toks * width // 128, 128)
    copies = jnp.broadcast_to(packed[None], (zs,) + packed.shape)
    column = lax.all_to_all(copies, "z", 0, 0, tiled=True)
    column = pl.pallas_call(
        spread_kernel,
        out_shape=jax.ShapeDtypeStruct((ys, mine, width), bf16),
        in_specs=[vmem, vmem],
        out_specs=vmem,
        scratch_shapes=[pltpu.VMEM((mine * width // 128, 128), f32)],
        compiler_params=pltpu.CompilerParams(vmem_limit_bytes=5 * 2**20),
        cost_estimate=pl.CostEstimate(flops=0, bytes_accessed=2**20, transcendentals=0),
        name="spread",
    )(column.reshape(mine * width // 128, 128), w_pair)

    products = pl.pallas_call(
        gains_kernel,
        out_shape=jax.ShapeDtypeStruct((8, 2 * ffn), f32),
        in_specs=[vmem] * 3,
        out_specs=vmem,
        compiler_params=pltpu.CompilerParams(vmem_limit_bytes=5 * 2**20),
        cost_estimate=pl.CostEstimate(flops=2**25, bytes_accessed=2 * 2**20, transcendentals=0),
        name="gains",
    )(gain, w_gate, w_up)
    flat = lax.all_to_all(column, "y", 0, 0, tiled=True).reshape(ys * mine, width)
    parts = pl.pallas_call(
        functools.partial(first_kernel, toks),
        out_shape=jax.ShapeDtypeStruct((mine + zs + 8, cols), bf16),
        in_specs=[vmem] * 5,
        out_specs=vmem,
        compiler_params=pltpu.CompilerParams(vmem_limit_bytes=6 * 2**20),
        cost_estimate=pl.CostEstimate(flops=2 * mine * width * cols, bytes_accessed=2 * 2**20, transcendentals=0),
        name="first",
    )(column, gain, products, w_first, w_pair)

    parts = lax.all_gather(parts, "core", axis=0, tiled=False)
    copies, mark = pl.pallas_call(
        functools.partial(combine_kernel, toks, width),
        out_shape=(
            jax.ShapeDtypeStruct((ns // 2,) + parts.shape[1:], bf16),
            jax.ShapeDtypeStruct((8, 128), f32),
        ),
        in_specs=[vmem],
        out_specs=(vmem, vmem),
        compiler_params=pltpu.CompilerParams(vmem_limit_bytes=5 * 2**20),
        cost_estimate=pl.CostEstimate(flops=2**24, bytes_accessed=2**20, transcendentals=0),
        name="combine",
    )(parts)

    sums = pl.pallas_call(
        hidden_kernel,
        out_shape=jax.ShapeDtypeStruct((ys * mine, 2 * ffn + 128), f32),
        in_specs=[anywhere] + [vmem] * 5,
        out_specs=anywhere,
        scratch_shapes=[
            pltpu.VMEM((ys * mine, width), bf16),
            pltpu.VMEM((ys * mine, 2 * ffn + 128), f32),
            pltpu.SemaphoreType.DMA((2,)),
            pltpu.SemaphoreType.DMA((2,)),
        ],
        compiler_params=pltpu.CompilerParams(vmem_limit_bytes=10 * 2**20),
        cost_estimate=pl.CostEstimate(flops=2**30, bytes_accessed=4 * 2**20, transcendentals=0),
        name="hidden",
    )(flat, gain, products, w_gate, w_up, mark)
    sums = lax.psum_scatter(sums, NARROW, scatter_dimension=0, tiled=True)

    parts = lax.all_to_all(copies, "x", 0, 0, tiled=True)
    notes = parts
    block = pl.pallas_call(
        functools.partial(second_kernel, toks, 2 * width),
        out_shape=jax.ShapeDtypeStruct((zs * 8, cols), bf16),
        in_specs=[vmem],
        out_specs=vmem,
        compiler_params=pltpu.CompilerParams(vmem_limit_bytes=6 * 2**20),
        cost_estimate=pl.CostEstimate(flops=2**24, bytes_accessed=2 * 2**20, transcendentals=0),
        name="second",
    )(parts)
    block = lax.all_to_all(block.reshape(zs, 8, cols), "z", 0, 0, tiled=True)

    block = pl.pallas_call(
        functools.partial(attend_kernel, new),
        out_shape=jax.ShapeDtypeStruct((zs * 8, cols), bf16),
        in_specs=[pl.BlockSpec(memory_space=pltpu.SMEM), vmem, vmem, vmem],
        out_specs=vmem,
        compiler_params=pltpu.CompilerParams(vmem_limit_bytes=6 * 2**20),
        cost_estimate=pl.CostEstimate(flops=2**28, bytes_accessed=2**20, transcendentals=2**16),
        name="attend",
    )(lengths, block.reshape(zs * 8, cols), key_cache, value_cache)
    block = block.reshape(zs, 8, cols)
    block = lax.all_to_all(block, "z", 0, 0, tiled=True)
    parts = jnp.concatenate([block[:, :toks].reshape(mine, cols), block[:, toks]], axis=0)
    parts = lax.all_gather(parts, NARROW, axis=0, tiled=False)
    hidden = pl.pallas_call(
        functools.partial(third_kernel, toks),
        out_shape=jax.ShapeDtypeStruct((sums.shape[0], ffn), bf16),
        in_specs=[vmem, vmem],
        out_specs=vmem,
        compiler_params=pltpu.CompilerParams(vmem_limit_bytes=5 * 2**20),
        cost_estimate=pl.CostEstimate(flops=2**24, bytes_accessed=2 * 2**20, transcendentals=0),
        name="third",
    )(sums, notes)
    hidden = lax.all_gather(hidden, NARROW, axis=0, tiled=True)
    down = jnp.dot(hidden, w_down, preferred_element_type=f32).astype(bf16)
    down = lax.all_to_all(down.reshape(ys, mine, width), "y", 0, 0, tiled=True)

    mixed = pl.pallas_call(
        functools.partial(last_kernel, toks, per_z),
        out_shape=jax.ShapeDtypeStruct((mine, width), bf16),
        in_specs=[vmem, vmem, vmem],
        out_specs=vmem,
        compiler_params=pltpu.CompilerParams(vmem_limit_bytes=6 * 2**20),
        cost_estimate=pl.CostEstimate(
            flops=2 * mine * width * cols, bytes_accessed=3 * 2**20, transcendentals=0
        ),
        name="last",
    )(parts, w_last, down)
    mixed = mixed.reshape(zs, toks * width // 128, 128)
    mixed = lax.all_to_all(mixed, "z", 0, 0, tiled=True)
    mixed = mixed.astype(f32).sum(0).reshape(toks, width)
    return (values + mixed).astype(bf16).reshape(activations.shape)


def solution(mesh):
    names = ("z", "y", "x", "core")
    split = Mesh(mesh.devices.reshape(16, 4, 4, 2), names)
    return jax.shard_map(
        local,
        mesh=split,
        in_specs=(
            P(WIDE, None, NARROW),
            P(NARROW),
            P(NARROW, WIDE),
            P(NARROW, WIDE),
            P(WIDE, NARROW),
            P(NARROW, WIDE),
            P(NARROW, WIDE),
            P(WIDE, NARROW),
            P(WIDE, NARROW, None),
            P(WIDE, NARROW, None),
            P(WIDE),
        ),
        out_specs=P(WIDE, None, NARROW),
        check_vma=False,
    )
```
